256 devices in a mesh: ctx: 8 (over x, core), head: 4 (over y), dp: 8 (over z).
Axes of the slice: x: 4, y: 4, z: 8, core: 2. Of those that a mesh axis runs over, the one named last changes fastest.
Arguments:
- student_q: bfloat16 [8, 2048, 3584], P('dp', 'ctx', 'head'), may hold values from -6 to 6
- student_k: bfloat16 [8, 2048, 3584], P('dp', 'ctx', 'head'), may hold values from -6 to 6
- student_v: bfloat16 [8, 2048, 3584], P('dp', 'ctx', 'head'), may hold values from -6 to 6
- beta: float32 [8, 28, 2048], P('dp', 'head', 'ctx'), may hold values from 0 to 0.95
- log_decay: float32 [8, 28, 2048], P('dp', 'head', 'ctx'), may hold values from -1 to 0
- kernel: float32 [8, 28, 4, 2048], P('dp', 'head', None, 'ctx'), may hold values from -3 to 3
- out_gain: float32 [3584], P('head'), may hold values from 0.1 to 1.9
- teacher_q: bfloat16 [8, 2048, 3584], P('dp', 'ctx', 'head'), may hold values from -8 to 8
- teacher_k: bfloat16 [8, 2048, 512], P('dp', 'ctx', 'head'), may hold values from -8 to 8
- teacher_v: bfloat16 [8, 2048, 512], P('dp', 'ctx', 'head'), may hold values from -6 to 6
- segment_ids: int32 [8, 2048], P('dp', 'ctx'), may hold values from 0 to 7, never falling along the last dimension, each value on 1 to 1024 neighbouring positions
- loss_weight: float32 [8, 28, 2048], P('dp', 'head', 'ctx'), may hold values from 0.05 to 40.5
Outputs:
- student_out: bfloat16 [8, 2048, 3584], P('dp', 'ctx', 'head')
- teacher_out: bfloat16 [8, 2048, 3584], P('dp', 'ctx', 'head')
- loss: float32 [], replicated
The draws below stay inside these ranges and needn't reach their ends.
All inputs are finite; a program needn't handle non-finite values.
Results may differ from the reference program's by a relative error of at most 0.0085.
Values may be sent and summed in bfloat16 or wider, within the bound.
No kernel may reach another device: no remote copies, remote signals or barrier semaphores. Data moves between devices by JAX's collectives and lax.ppermute only.
A program may use at most 128 MiB of HBM per device.

```python
import math
import jax
import jax.numpy as jnp
import numpy as np
from jax import lax

HEADS = 28
KVH = 4
DK = 128
TOK_DEV = 256
SPAN = 64
TAPS = 4
DOCS = 8
TOKEN_SPAN_SIZE = 2048
STREAM_COUNT_ALL = 8
N_CTX = 8


def draw_teacher_q(key, part):
    key = jax.random.fold_in(key, 11)
    return jnp.clip(jax.random.normal(key, (STREAM_COUNT_ALL, TOKEN_SPAN_SIZE, HEADS * DK), jnp.float32), -8.0, 8.0).astype(jnp.bfloat16)


def draw_teacher_k(key, part):
    key = jax.random.fold_in(key, 12)
    return jnp.clip(jax.random.normal(key, (STREAM_COUNT_ALL, TOKEN_SPAN_SIZE, KVH * DK), jnp.float32), -8.0, 8.0).astype(jnp.bfloat16)


def draw_beta(key, part):
    key = jax.random.fold_in(key, 3)
    first_key, second_key = jax.random.split(key)
    lowest = 0.1 * DK / TOKEN_SPAN_SIZE
    highest = 0.6
    levels = jnp.exp(jax.random.uniform(first_key, (STREAM_COUNT_ALL, HEADS, 1), jnp.float32, math.log(lowest), math.log(highest)))
    jitter = jax.random.uniform(second_key, (STREAM_COUNT_ALL, HEADS, TOKEN_SPAN_SIZE), jnp.float32, 0.5, 1.5)
    return jnp.minimum(levels * jitter, 0.95)


def draw_log_decay(key, part):
    key = jax.random.fold_in(key, 2)
    boundary_flag_seed, rapid_change_seed, slow_drift_seed, perturbation_seed, placement_seed, spike_prng_seed = jax.random.split(key, 6)
    share = 0.5
    is_fast = jax.random.uniform(boundary_flag_seed, (STREAM_COUNT_ALL, HEADS, 1), jnp.float32) < share
    fast_rate = 1.0 / jax.random.uniform(rapid_change_seed, (STREAM_COUNT_ALL, HEADS, 1), jnp.float32, 30.0, 50.0)
    slow_rate = jax.random.uniform(slow_drift_seed, (STREAM_COUNT_ALL, HEADS, 1), jnp.float32, 0.1, 1.0) * 0.5 / TOKEN_SPAN_SIZE
    rates = jnp.where(is_fast, fast_rate, slow_rate)
    jitter = jax.random.uniform(perturbation_seed, (STREAM_COUNT_ALL, HEADS, TOKEN_SPAN_SIZE), jnp.float32, 0.5, 2.0)
    places = jax.random.randint(placement_seed, (STREAM_COUNT_ALL, 1, 4), 0, TOKEN_SPAN_SIZE)
    hits = jnp.any(jnp.arange(TOKEN_SPAN_SIZE)[None, :, None] == places, axis=-1)
    draw_amounts = jnp.log(jax.random.uniform(spike_prng_seed, (STREAM_COUNT_ALL, 1, TOKEN_SPAN_SIZE), jnp.float32, 0.5, 0.8))
    return -rates * jitter + jnp.where(hits[:, None, :], draw_amounts, 0.0)


def draw_loss_weight(key, part):
    key = jax.random.fold_in(key, 5)
    first_key, second_key = jax.random.split(key)
    position = jnp.arange(TOKEN_SPAN_SIZE, dtype=jnp.float32) / (TOKEN_SPAN_SIZE - 1)
    row_scale = jnp.exp(jax.random.uniform(first_key, (STREAM_COUNT_ALL, HEADS, 1), jnp.float32, math.log(0.1), math.log(1.0)))
    rising = 1.0 + 2.0 * position
    jitter = jax.random.uniform(second_key, (STREAM_COUNT_ALL, HEADS, TOKEN_SPAN_SIZE), jnp.float32, 0.5, 1.5)
    return row_scale * rising[None, None, :] * jitter


def block_scale(rng, dims, shards, low, high):
    gain = 1.0
    for axis_at, shards_of in shards:
        heights = jax.random.uniform(jax.random.fold_in(jax.random.fold_in(rng, 6), axis_at), (shards_of,), jnp.float32, low / len(shards), high / len(shards))
        gain = gain * jnp.repeat(jnp.exp(heights), dims[axis_at] // shards_of).reshape((-1,) + (1,) * (len(dims) - 1 - axis_at))
    return gain


def profile(count, total, most, slope):
    loads = [(1 << 20) // math.isqrt(standing ** slope) + 1 for standing in range(2, count + 1)]
    spare, counts = total - most - (count - 1), [1] * (count - 1)
    while spare > 0:
        free = [i for i in range(count - 1) if counts[i] < most]
        pool, remaining = sum([loads[i] for i in free]), spare
        for i in free:
            extra = min(most - counts[i], max(1, remaining * loads[i] // pool), spare)
            counts[i] = counts[i] + extra
            spare = spare - extra
    return np.array([most] + counts)


def ragged(rng, number_of, total, bound, slope):
    if number_of == 2:
        one = jax.random.randint(rng, (), max(1, total - bound), min(bound, total - 1) + 1)
        return jnp.stack([one, total - one])
    lengths = jnp.asarray(profile(number_of, total, bound, slope), jnp.int32)
    couples = (number_of - 1) // 2
    donor, receiver = lengths[1:1 + 2 * couples:2], lengths[2:2 + 2 * couples:2]
    margin = jnp.minimum(donor - 1, bound - receiver)
    moved = jax.random.randint(jax.random.fold_in(rng, 1), (couples,), 0, 1 << 20) % (margin + 1)
    lengths = lengths.at[1:1 + 2 * couples:2].set(donor - moved).at[2:2 + 2 * couples:2].set(receiver + moved)
    return lengths[jax.random.permutation(jax.random.fold_in(rng, 2), number_of)]


def normal_values(key, dims, scale, limit, cuts=(), kind=jnp.bfloat16):
    factor_of = block_scale(key, dims, cuts, -0.22, 0.18) if cuts else 1.0
    values = jax.random.normal(key, dims, jnp.float32) * scale * factor_of
    return jnp.minimum(jnp.maximum(values, -limit), limit).astype(kind)


def setup_inputs(seed: int = 0) -> dict:
    keys = jax.random.split(jax.random.key(seed), 13)
    return {
        "student_q": normal_values(keys[0], (STREAM_COUNT_ALL, TOKEN_SPAN_SIZE, HEADS * DK), 1.0, 6.0, ((0, 8), (1, 8), (2, 4))),
        "student_k": normal_values(keys[1], (STREAM_COUNT_ALL, TOKEN_SPAN_SIZE, HEADS * DK), 1.0, 6.0, ((0, 8), (1, 8), (2, 4))),
        "student_v": normal_values(keys[2], (STREAM_COUNT_ALL, TOKEN_SPAN_SIZE, HEADS * DK), 1.0, 6.0, ((0, 8), (1, 8), (2, 4))),
        "beta": draw_beta(jax.random.fold_in(keys[12], 71), 0),
        "log_decay": draw_log_decay(jax.random.fold_in(keys[12], 71), 0),
        "kernel": normal_values(keys[5], (STREAM_COUNT_ALL, HEADS, TAPS, TOKEN_SPAN_SIZE), 0.6, 3.0, ((0, 8), (1, 4), (3, 8)), jnp.float32),
        "out_gain": jnp.clip(1.0 + 0.18 * jax.random.normal(keys[6], (HEADS * DK,), jnp.float32), 0.1, 1.9),
        "teacher_q": draw_teacher_q(jax.random.fold_in(keys[12], 71), 0),
        "teacher_k": draw_teacher_k(jax.random.fold_in(keys[12], 71), 0),
        "teacher_v": normal_values(keys[9], (STREAM_COUNT_ALL, TOKEN_SPAN_SIZE, KVH * DK), 1.0, 6.0, ((0, 8), (1, 8), (2, 4))),
        "segment_ids": jax.vmap(lambda own: jnp.searchsorted(jnp.cumsum(ragged(own, DOCS, TOKEN_SPAN_SIZE, TOK_DEV * N_CTX // 2, 0)), jnp.arange(TOKEN_SPAN_SIZE), side="right"))(jax.random.split(keys[10], STREAM_COUNT_ALL)).reshape((STREAM_COUNT_ALL, TOKEN_SPAN_SIZE)).astype(jnp.int32),
        "loss_weight": draw_loss_weight(jax.random.fold_in(keys[12], 71), 0),
    }


PRECISE = lax.Precision.HIGHEST
EPSILON = 1e-06
MASKED = -1e+30

def matmul(left, right):
    return jnp.dot(left, right, precision=PRECISE)

def unit_rows(matrix):
    return matrix * lax.rsqrt(lax.optimization_barrier(jnp.sum(matrix * matrix, axis=-1, keepdims=True)) + EPSILON)

def span_terms(query_rows, key_rows, value_rows, beta_rows, decay_rows, segment_rows, previous):
    length = query_rows.shape[0]
    head_dim = key_rows.shape[1]
    row_index = lax.broadcasted_iota(jnp.int32, (length, length), 0)
    col_index = lax.broadcasted_iota(jnp.int32, (length, length), 1)
    running = jnp.cumsum(decay_rows)
    same_doc = segment_rows[:, None] == segment_rows[None, :]
    reachable = (col_index <= row_index) & same_doc
    between = jnp.exp(jnp.minimum(running[:, None] - running[None, :], 0.0))
    between = jnp.where(reachable, between, 0.0)
    from_start = jnp.where(segment_rows == previous, jnp.exp(running), 0.0)
    weighted = between * beta_rows[None, :]
    coupling = jnp.where(col_index < row_index, weighted * matmul(key_rows, key_rows.T), 0.0)
    reading = weighted * matmul(query_rows, key_rows.T)
    identity_small = jnp.eye(length, dtype=jnp.float32)
    power_term = -coupling
    inverse = identity_small + power_term
    for doubling in range(1, (length - 1).bit_length()):
        power_term = matmul(power_term, power_term)
        inverse = matmul(inverse, identity_small + power_term)
    fresh_values = matmul(inverse, value_rows)
    carried = matmul(inverse, from_start[:, None] * key_rows)
    end_keys = weighted[length - 1][:, None] * key_rows
    transition = from_start[length - 1] * jnp.eye(head_dim, dtype=jnp.float32) - matmul(end_keys.T, carried)
    injection = matmul(end_keys.T, fresh_values)
    local_part = matmul(reading, fresh_values)
    state_reader = from_start[:, None] * query_rows - matmul(reading, carried)
    return (transition, injection, local_part, state_reader)

def convolve(values, kernel, segments):
    length = values.shape[0]
    convolved = jnp.zeros_like(values)
    for offset in range(TAPS):
        shifted = jnp.pad(values, ((offset, 0), (0, 0), (0, 0)))[:length]
        moved_ids = jnp.pad(segments, (offset, 0), constant_values=-1)[:length]
        keep_mask = (moved_ids == segments).astype(jnp.float32)
        convolved = convolved + jnp.transpose(kernel[:, offset, :])[:, :, None] * keep_mask[:, None, None] * shifted
    return jax.nn.silu(convolved)

def teacher_head(query_rows, key_rows, value_rows, segments):
    length = query_rows.shape[0]
    row_index = lax.broadcasted_iota(jnp.int32, (length, length), 0)
    col_index = lax.broadcasted_iota(jnp.int32, (length, length), 1)
    scores = jnp.dot(query_rows, key_rows.T, preferred_element_type=jnp.float32) * DK ** (-0.5)
    visible = (col_index <= row_index) & (segments[:, None] == segments[None, :])
    largest = lax.optimization_barrier(jnp.max(jnp.where(visible, scores, MASKED), axis=1, keepdims=True))
    weights = jnp.where(visible, jnp.exp(scores - largest), 0.0)
    denominator = lax.optimization_barrier(jnp.sum(weights, axis=1, keepdims=True))
    return jnp.dot(weights.astype(jnp.bfloat16), value_rows, preferred_element_type=jnp.float32) / denominator

def reference(student_q, student_k, student_v, beta, log_decay, kernel, out_gain, teacher_q, teacher_k, teacher_v, segment_ids, loss_weight):
    batch, length, features = student_q.shape
    count = length // SPAN
    queries = unit_rows(student_q.astype(jnp.float32).reshape(batch, length, HEADS, DK))
    keys_unit = unit_rows(student_k.astype(jnp.float32).reshape(batch, length, HEADS, DK))
    values = jax.vmap(convolve)(student_v.astype(jnp.float32).reshape(batch, length, HEADS, DK), kernel, segment_ids)

    def by_span(matrix):
        return jnp.transpose(matrix.reshape(batch, count, SPAN, HEADS, DK), (1, 0, 3, 2, 4))

    def by_span_rows(matrix):
        return jnp.transpose(matrix.reshape(batch, HEADS, count, SPAN), (2, 0, 1, 3))
    segment_spans = jnp.transpose(segment_ids.reshape(batch, count, SPAN), (1, 0, 2))
    previous_ids = jnp.concatenate([jnp.full((batch, 1), -1, jnp.int32), segment_ids[:, :-1]], axis=1)
    previous_spans = jnp.transpose(previous_ids.reshape(batch, count, SPAN)[:, :, 0], (1, 0))
    over_heads = jax.vmap(span_terms, in_axes=(0, 0, 0, 0, 0, None, None))
    over_all = jax.vmap(over_heads)

    def advance(state_now, bundle):
        transition, injection, local_part, state_reader = over_all(*bundle)
        produced = local_part + jnp.einsum('bhck,bhkv->bhcv', state_reader, state_now, precision=PRECISE)
        state_next = jnp.einsum('bhij,bhjv->bhiv', transition, state_now, precision=PRECISE) + injection
        return (state_next, produced)
    initial = jnp.zeros((batch, HEADS, DK, DK), jnp.float32)
    _, produced = lax.scan(advance, initial, (by_span(queries), by_span(keys_unit), by_span(values), by_span_rows(beta), by_span_rows(log_decay), segment_spans, previous_spans))
    student = jnp.transpose(produced, (1, 2, 0, 3, 4)).reshape(batch, HEADS, length, DK)
    gains = out_gain.reshape(HEADS, DK)[None, :, None, :]
    student = student * lax.rsqrt(lax.optimization_barrier(jnp.mean(student * student, axis=-1, keepdims=True)) + EPSILON) * gains
    per_group = HEADS // KVH
    heads_q = jnp.transpose(teacher_q.reshape(batch, length, HEADS, DK), (0, 2, 1, 3))
    heads_k = jnp.transpose(teacher_k.reshape(batch, length, KVH, DK), (0, 2, 1, 3))
    heads_v = jnp.transpose(teacher_v.reshape(batch, length, KVH, DK), (0, 2, 1, 3))

    def one_sequence(bundle):
        seq_q, seq_k, seq_v, segments = bundle

        def one_head(head_index):
            return teacher_head(seq_q[head_index], seq_k[head_index // per_group], seq_v[head_index // per_group], segments)
        return lax.map(one_head, jnp.arange(HEADS))
    teacher = lax.map(one_sequence, (heads_q, heads_k, heads_v, segment_ids))
    difference = student - teacher
    errors = lax.optimization_barrier(jnp.mean(difference * difference, axis=-1))
    loss = jnp.sum(loss_weight * errors) / (batch * HEADS * length)
    student_out = jnp.transpose(student, (0, 2, 1, 3)).reshape(batch, length, HEADS * DK).astype(jnp.bfloat16)
    teacher_out = jnp.transpose(teacher, (0, 2, 1, 3)).reshape(batch, length, HEADS * DK).astype(jnp.bfloat16)
    return (student_out, teacher_out, loss)
```

```python
import math

import jax
import jax.numpy as jnp
from jax import lax
from jax.experimental import pallas as pl
from jax.experimental.pallas import tpu as pltpu
from jax.sharding import PartitionSpec as P

EPSILON = 1e-06
MASKED = -1e30
HEAD = 128
F32 = jnp.float32
BF16 = jnp.bfloat16
VMEM_BYTES = 32 * 1024 * 1024


def nn(a, b, precision=None):
    return lax.dot_general(
        a, b, (((1,), (0,)), ((), ())), precision=precision, preferred_element_type=F32
    )


def nt(a, b):
    return lax.dot_general(a, b, (((1,), (1,)), ((), ())), preferred_element_type=F32)


def tn(a, b):
    return lax.dot_general(a, b, (((0,), (0,)), ((), ())), preferred_element_type=F32)


def head_lanes(h):
    return slice(h * HEAD, (h + 1) * HEAD)


def call(body, outs, *args, scratch=(), flops=0):
    return pl.pallas_call(
        body,
        out_shape=[jax.ShapeDtypeStruct(s, d) for s, d in outs],
        in_specs=[pl.BlockSpec(memory_space=pltpu.VMEM)] * len(args),
        out_specs=[pl.BlockSpec(memory_space=pltpu.VMEM)] * len(outs),
        scratch_shapes=[pltpu.VMEM(s, d) for s, d in scratch],
        compiler_params=pltpu.CompilerParams(vmem_limit_bytes=VMEM_BYTES),
        cost_estimate=pl.CostEstimate(flops=flops, bytes_accessed=0, transcendentals=0),
    )(*args)


def pack_body(tk, tv, sv, ids, kv, rim):
    tokens = tk.shape[1]
    kv[0:tokens] = tk[0]
    kv[tokens : 2 * tokens] = tv[0]
    idf = ids[...].astype(F32)
    rows = lax.broadcasted_iota(jnp.int32, (16, 128), 0)
    block = jnp.zeros((16, 128), F32)
    for i in range(tokens // 128):
        block = jnp.where(rows == i, idf[:, i * 128 : (i + 1) * 128], block)
    kv[2 * tokens : 2 * tokens + 16] = block.astype(BF16)
    features = sv.shape[2]
    rim[:, 0:features] = sv[0, tokens - 16 : tokens, :]
    rim[:, features : features + 128] = jnp.broadcast_to(
        idf[:, tokens - 128 : tokens], (16, 128)
    ).astype(BF16)


def keys_body(k, beta, decay, ids, t_out, uk_out, kend_out, m_out, rows_out, cols_out, eight, a_s, t_s):
    tokens = k.shape[1]
    heads = beta.shape[1]
    half = tokens // 2
    idf = ids[...].astype(F32)
    lane = lax.broadcasted_iota(jnp.int32, (tokens, 128), 1)
    packed = jnp.zeros((tokens, 128), F32)
    for h in range(heads):
        kf = k[0, :, head_lanes(h)].astype(F32)
        norm = lax.rsqrt(jnp.sum(kf * kf, axis=1, keepdims=True) + EPSILON)
        packed = jnp.where(lane == h, norm, packed)
    r8 = packed.T[0:8]
    eight[...] = jnp.zeros_like(eight)
    eight[0, 0:heads] = decay[0]
    eight[1, 0:heads] = beta[0]
    row_index = lax.broadcasted_iota(jnp.int32, (tokens, tokens), 0)
    col_index = lax.broadcasted_iota(jnp.int32, (tokens, tokens), 1)
    upto = jnp.where(row_index <= col_index, 1.0, 0.0)
    run8 = nn(eight[0], upto, lax.Precision.HIGHEST)
    br8 = eight[1] * r8
    fs8 = jnp.where(idf == idf[:, 0:1], jnp.exp(run8), 0.0)
    wend8 = (
        jnp.where(
            idf == idf[:, tokens - 1 : tokens],
            jnp.exp(run8[:, tokens - 1 : tokens] - run8),
            0.0,
        )
        * br8
    )
    ids8 = jnp.broadcast_to(idf, (8, tokens))
    rows_out[...] = jnp.concatenate([run8, br8], axis=0)
    stacked = jnp.concatenate(
        [run8, wend8, fs8 * r8, fs8, ids8, r8, jnp.zeros((80, tokens), F32)], axis=0
    )
    cols = stacked.T
    cols_out[...] = cols
    visible = (col_index < row_index) & (cols[:, 32:33] == idf)
    for h in range(heads):
        kh = k[0, :, head_lanes(h)]
        kk = nt(kh, kh)
        between = jnp.where(visible, jnp.exp(cols[:, h : h + 1] - run8[h : h + 1]), 0.0)
        a = between * br8[h : h + 1] * (cols[:, 40 + h : 41 + h] * kk)
        a_s[h] = a.astype(BF16)
    ri = lax.broadcasted_iota(jnp.int32, (half, half), 0)
    ci = lax.broadcasted_iota(jnp.int32, (half, half), 1)
    eye = jnp.where(ri == ci, 1.0, 0.0)

    def level_mask(k_bits):
        rb, cb = ri >> k_bits, ci >> k_bits
        return jnp.where(((rb & 1) == 1) & (cb == rb - 1), 1.0, 0.0)

    def diag(h, b):
        return a_s[h, b * half : (b + 1) * half, b * half : (b + 1) * half]

    first = level_mask(0)
    for h in range(heads):
        for b in range(2):
            t_s[2 * h + b] = eye - diag(h, b).astype(F32) * first
    for bits in range(1, (half - 1).bit_length()):
        mask = level_mask(bits).astype(BF16)
        for h in range(heads):
            for b in range(2):
                t = t_s[2 * h + b]
                tb = t.astype(BF16)
                p = nn(diag(h, b) * mask, tb)
                t_s[2 * h + b] = t - nn(tb, p.astype(BF16))
    for h in range(heads):
        t11 = t_s[2 * h].astype(BF16)
        t22 = t_s[2 * h + 1].astype(BF16)
        p = nn(a_s[h, half:tokens, 0:half], t11)
        t_out[h, 0:half, 0:half] = t11
        t_out[h, half:tokens, half:tokens] = t22
        t_out[h, 0:half, half:tokens] = jnp.zeros((half, half), BF16)
        t_out[h, half:tokens, 0:half] = (-nn(t22, p.astype(BF16))).astype(BF16)
    er = lax.broadcasted_iota(jnp.int32, (HEAD, HEAD), 0)
    ec = lax.broadcasted_iota(jnp.int32, (HEAD, HEAD), 1)
    for h in range(heads):
        kf = k[0, :, head_lanes(h)].astype(F32)
        uk = nn(t_out[h], (cols[:, 16 + h : 17 + h] * kf).astype(BF16)).astype(BF16)
        uk_out[h] = uk
        kend = (cols[:, 8 + h : 9 + h] * kf).astype(BF16)
        kend_out[h] = kend
        scale = fs8[h : h + 1, tokens - 1 : tokens]
        m_out[h] = jnp.where(er == ec, scale, 0.0) - tn(kend, uk)


def values_body(v, rim, taps, ids, t, kend, m, mi_out, uv_out, x_s, tap_s):
    tokens = v.shape[1]
    features = v.shape[2]
    heads = taps.shape[1]
    count = taps.shape[2]
    first = lax.axis_index("ctx") == 0
    idf = ids[...].astype(F32)
    before = rim[0:1, features : features + 128].astype(F32)
    before = jnp.where(first, -1.0, before)
    longer = jnp.concatenate([before, idf], axis=1)
    keeps = [
        (pltpu.roll(longer, j, 1)[:, 128:] == idf).astype(F32) if j else jnp.ones_like(idf)
        for j in range(count)
    ]
    keep = jnp.concatenate(keeps, axis=0)
    tap_s[...] = jnp.zeros_like(tap_s)
    for h in range(heads):
        tap_s[8 * h : 8 * h + count] = taps[0, h] * keep
    cols = tap_s[...].T
    x_s[0:8] = rim[:, 0:features].astype(F32)[8:16]
    x_s[8 : 8 + tokens] = v[0].astype(F32)
    joined = jnp.where(before[0:1, 127:128] == idf[:, 0:1], 1.0, 0.0)
    for h in range(heads):
        conv = cols[:, 8 * h : 8 * h + 1] * x_s[8 : 8 + tokens, head_lanes(h)]
        for j in range(1, count):
            conv = conv + cols[:, 8 * h + j : 8 * h + j + 1] * x_s[8 - j : 8 - j + tokens, head_lanes(h)]
        values = conv / (1.0 + jnp.exp(-conv))
        uv = nn(t[h], values.astype(BF16)).astype(BF16)
        uv_out[h] = uv
        mi_out[h] = (joined * m[h]).astype(BF16)
        mi_out[heads + h] = tn(kend[h], uv).astype(BF16)


def queries_body(q, k, rim, ids, rows, cols_in, uk, uv, lw, local_out, reader_out, lw_out, lw_s):
    tokens = q.shape[1]
    features = q.shape[2]
    heads = uk.shape[0]
    first = lax.axis_index("ctx") == 0
    idf = ids[...].astype(F32)
    before = jnp.where(first, -1.0, rim[0:1, features : features + 128].astype(F32))
    joined = jnp.where(before[0:1, 127:128] == idf[:, 0:1], 1.0, 0.0)
    row_index = lax.broadcasted_iota(jnp.int32, (tokens, tokens), 0)
    col_index = lax.broadcasted_iota(jnp.int32, (tokens, tokens), 1)
    cols = cols_in[...]
    visible = (col_index <= row_index) & (cols[:, 32:33] == idf)
    lw_s[...] = jnp.zeros_like(lw_s)
    lw_s[0:heads] = lw[0]
    lw_out[...] = lw_s[...].T
    for h in range(heads):
        qh = q[0, :, head_lanes(h)]
        qf = qh.astype(F32)
        norm = lax.rsqrt(jnp.sum(qf * qf, axis=1, keepdims=True) + EPSILON)
        qk = nt(qh, k[0, :, head_lanes(h)])
        between = jnp.where(visible, jnp.exp(cols[:, h : h + 1] - rows[h : h + 1]), 0.0)
        reading = (between * rows[8 + h : 9 + h] * (norm * qk)).astype(BF16)
        local_out[h] = nn(reading, uv[h])
        carried = nn(reading, uk[h])
        reader = (cols[:, 24 + h : 25 + h] * norm) * qf - carried
        reader_out[h] = (joined * reader).astype(BF16)


def teacher_body(q, ids, own, r2, r4, x0, x2, x4, out, full, k_s, v_s, id_s, bias_s):
    tokens = q.shape[1]
    heads = q.shape[2] // HEAD
    halves = tokens // 128
    index = lax.axis_index("ctx")
    odd = lax.rem(index, 2) == 1
    idf = ids[...].astype(F32)

    def place(slot, source):
        k_s[slot * tokens : (slot + 1) * tokens] = source[0:tokens]
        v_s[slot * tokens : (slot + 1) * tokens] = source[tokens : 2 * tokens]
        behind = 4 - slot
        valid = index >= behind
        names = source[2 * tokens : 2 * tokens + 16].astype(F32)
        for i in range(halves):
            at = (slot * halves + i) * 128
            id_s[:, at : at + 128] = jnp.where(valid, names[i : i + 1], -1.0)

    place(0, r4)
    place(2, r2)
    place(4, own)

    @pl.when(odd)
    def _():
        place(1, x2)
        place(3, x0)

    @pl.when(jnp.logical_not(odd))
    def _():
        place(1, x4)
        place(3, x2)

    width = 5 * tokens
    id_col = jnp.broadcast_to(idf, (128, tokens)).T[:, 0:1]
    same = id_col == id_s[...]
    row_index = lax.broadcasted_iota(jnp.int32, (tokens, width), 0)
    col_index = lax.broadcasted_iota(jnp.int32, (tokens, width), 1) - 4 * tokens
    bias_s[...] = jnp.where(same & (col_index <= row_index), 0.0, MASKED)
    scale = math.log2(math.e) / math.sqrt(HEAD)
    span = width - (halves - 1) * 128
    for h in range(heads):
        for r in range(halves):
            qt = q[0, r * 128 : (r + 1) * 128, head_lanes(h)]
            s = nt(qt, k_s[r * 128 : r * 128 + span])
            s = s * scale + bias_s[r * 128 : (r + 1) * 128, r * 128 : r * 128 + span]
            largest = jnp.max(s, axis=1, keepdims=True)
            w = jnp.exp2(s - largest)
            total = jnp.sum(w, axis=1, keepdims=True)
            o = nn(w.astype(BF16), v_s[r * 128 : r * 128 + span]) / total
            full[r * 128 : (r + 1) * 128, head_lanes(h)] = o
            out[0, r * 128 : (r + 1) * 128, head_lanes(h)] = o.astype(BF16)


def chip_body(own, other, m_out, i_out):
    heads = m_out.shape[0]
    odd = lax.rem(lax.axis_index("ctx"), 2) == 1
    for h in range(heads):
        m_own, m_other = own[h], other[h]
        i_own, i_other = own[heads + h], other[heads + h]
        later_m = jnp.where(odd, m_own, m_other)
        later_i = jnp.where(odd, i_own, i_other)
        early_m = jnp.where(odd, m_other, m_own)
        early_i = jnp.where(odd, i_other, i_own)
        m_out[h] = nn(later_m, early_m).astype(BF16)
        i_out[h] = (nn(later_m, early_i) + later_i.astype(F32)).astype(BF16)


def join_body(m, i, arriving, out):
    for h in range(m.shape[0]):
        out[h] = (nn(m[h], arriving[h]) + i[h].astype(F32)).astype(BF16)


def finish_body(arriving, other, local, reader, gain, teacher, lw, out, sums):
    heads = arriving.shape[0]
    odd = lax.rem(lax.axis_index("ctx"), 2) == 1
    total = jnp.zeros(teacher[:, 0:HEAD].shape, F32)
    for h in range(heads):
        s = arriving[h]
        stepped = (nn(other[h], s) + other[heads + h].astype(F32)).astype(BF16)
        s = jnp.where(odd, stepped, s)
        o = local[h] + nn(reader[h], s)
        mean = jnp.sum(o * o, axis=1, keepdims=True) * (1.0 / HEAD)
        student = o * lax.rsqrt(mean + EPSILON) * gain[:, head_lanes(h)]
        out[0, :, head_lanes(h)] = student.astype(BF16)
        difference = student - teacher[:, head_lanes(h)]
        total = total + lw[:, h : h + 1] * (difference * difference)
    partial = jnp.sum(jnp.sum(total, axis=0, keepdims=True), axis=1, keepdims=True)
    sums[...] = jnp.broadcast_to(partial, sums.shape)


def on_device(
    student_q,
    student_k,
    student_v,
    beta,
    log_decay,
    kernel,
    out_gain,
    teacher_q,
    teacher_k,
    teacher_v,
    segment_ids,
    loss_weight,
):
    _, tokens, features = student_q.shape
    heads = beta.shape[1]
    shards = lax.axis_size("ctx")
    everyone = shards * lax.axis_size("head") * lax.axis_size("dp")

    def rotated(block, distance):
        return lax.ppermute(block, "ctx", [(i, (i + distance) % shards) for i in range(shards)])

    def swapped(block):
        return lax.ppermute(block, "ctx", [(i, i ^ 1) for i in range(shards)])

    kv, rim = call(
        pack_body,
        [((2 * tokens + 16, HEAD), BF16), ((16, features + 128), BF16)],
        teacher_k,
        teacher_v,
        student_v,
        segment_ids,
    )
    rim = rotated(rim, 1)
    r2 = rotated(kv, 2)
    r4 = rotated(kv, 4)
    t, uk, kend, m0, rows, cols = call(
        keys_body,
        [
            ((heads, tokens, tokens), BF16),
            ((heads, tokens, HEAD), BF16),
            ((heads, tokens, HEAD), BF16),
            ((heads, HEAD, HEAD), F32),
            ((16, tokens), F32),
            ((tokens, 128), F32),
        ],
        student_k,
        beta,
        log_decay,
        segment_ids,
        scratch=[
            ((2, 8, tokens), F32),
            ((heads, tokens, tokens), BF16),
            ((2 * heads, tokens // 2, tokens // 2), F32),
        ],
        flops=4 * 10**9,
    )
    mi, uv = call(
        values_body,
        [((2 * heads, HEAD, HEAD), BF16), ((heads, tokens, HEAD), BF16)],
        student_v,
        rim,
        kernel,
        segment_ids,
        t,
        kend,
        m0,
        scratch=[((8 + tokens, features), F32), ((128, tokens), F32)],
        flops=2 * 10**9,
    )
    mi_other = swapped(mi)
    local, reader, lw = call(
        queries_body,
        [
            ((heads, tokens, HEAD), F32),
            ((heads, tokens, HEAD), BF16),
            ((tokens, 128), F32),
        ],
        student_q,
        student_k,
        rim,
        segment_ids,
        rows,
        cols,
        uk,
        uv,
        loss_weight,
        scratch=[((128, tokens), F32)],
        flops=2 * 10**9,
    )
    x0, x2, x4 = swapped(kv), swapped(r2), swapped(r4)
    m_chip, i_chip = call(
        chip_body,
        [((heads, HEAD, HEAD), BF16), ((heads, HEAD, HEAD), BF16)],
        mi,
        mi_other,
        flops=10**8,
    )
    behind = rotated(i_chip, 2)
    teacher_out, teacher = call(
        teacher_body,
        [((1, tokens, features), BF16), ((tokens, features), F32)],
        teacher_q,
        segment_ids,
        kv,
        r2,
        r4,
        x0,
        x2,
        x4,
        scratch=[
            ((5 * tokens, HEAD), BF16),
            ((5 * tokens, HEAD), BF16),
            ((1, 5 * tokens), F32),
            ((tokens, 5 * tokens), F32),
        ],
        flops=5 * 10**9,
    )
    (joined,) = call(
        join_body, [((heads, HEAD, HEAD), BF16)], m_chip, i_chip, behind, flops=10**8
    )
    arriving = rotated(joined, 2)
    student_out, sums = call(
        finish_body,
        [((1, tokens, features), BF16), ((everyone, 128), F32)],
        arriving,
        mi_other,
        local,
        reader,
        out_gain.reshape(1, features),
        teacher,
        lw,
        flops=10**9,
    )
    gathered = lax.all_to_all(sums, ("ctx", "head", "dp"), 0, 0, tiled=True)
    loss = jnp.sum(gathered[:, 0]) / (everyone * heads * tokens * HEAD)
    return (student_out, teacher_out, loss)


def solution(mesh):
    placed = (
        P("dp", "ctx", "head"),
        P("dp", "ctx", "head"),
        P("dp", "ctx", "head"),
        P("dp", "head", "ctx"),
        P("dp", "head", "ctx"),
        P("dp", "head", None, "ctx"),
        P("head"),
        P("dp", "ctx", "head"),
        P("dp", "ctx", "head"),
        P("dp", "ctx", "head"),
        P("dp", "ctx"),
        P("dp", "head", "ctx"),
    )
    return jax.shard_map(
        on_device,
        mesh=mesh,
        in_specs=placed,
        out_specs=(P("dp", "ctx", "head"), P("dp", "ctx", "head"), P()),
        check_vma=False,
    )
```

```python
import functools
import math

import jax
import jax.numpy as jnp
from jax import lax
from jax.experimental import pallas as pl
from jax.experimental.pallas import tpu as pltpu
from jax.sharding import PartitionSpec as P

EPSILON = 1e-06
MASKED = -1e30
HEAD = 128
F32 = jnp.float32
BF16 = jnp.bfloat16
VMEM_BYTES = 32 * 1024 * 1024
PACK_VMEM = 62 * 1024 * 1024


def nn(a, b, precision=None):
    return lax.dot_general(
        a, b, (((1,), (0,)), ((), ())), precision=precision, preferred_element_type=F32
    )


def nt(a, b):
    return lax.dot_general(a, b, (((1,), (1,)), ((), ())), preferred_element_type=F32)


def tn(a, b):
    return lax.dot_general(a, b, (((0,), (0,)), ((), ())), preferred_element_type=F32)


def head_lanes(h):
    return slice(h * HEAD, (h + 1) * HEAD)


def call(body, outs, *args, scratch=(), hbm=(), flops=0, vmem=VMEM_BYTES):
    buffers = [pltpu.VMEM(s, d) for s, d in scratch]
    if hbm:
        buffers.append(pltpu.SemaphoreType.DMA((len(hbm),)))
    return pl.pallas_call(
        body,
        out_shape=[jax.ShapeDtypeStruct(s, d) for s, d in outs],
        in_specs=[
            pl.BlockSpec(memory_space=pltpu.HBM if i in hbm else pltpu.VMEM)
            for i in range(len(args))
        ],
        out_specs=[pl.BlockSpec(memory_space=pltpu.VMEM)] * len(outs),
        scratch_shapes=buffers,
        compiler_params=pltpu.CompilerParams(vmem_limit_bytes=vmem),
        cost_estimate=pl.CostEstimate(flops=flops, bytes_accessed=0, transcendentals=0),
    )(*args)


def pack_body(tk, tv, sv, ids, kv, rim, id_s, sems):
    tokens = tk.shape[1]
    features = sv.shape[2]
    moves = [
        pltpu.make_async_copy(ids, id_s, sems.at[0]),
        pltpu.make_async_copy(
            sv.at[0, tokens - 16 : tokens, :], rim.at[:, 0:features], sems.at[1]
        ),
        pltpu.make_async_copy(tk.at[0], kv.at[0:tokens], sems.at[2]),
        pltpu.make_async_copy(tv.at[0], kv.at[tokens : 2 * tokens], sems.at[3]),
    ]
    for move in moves:
        move.start()
    moves[0].wait()
    idf = id_s[...].astype(F32)
    rows = lax.broadcasted_iota(jnp.int32, (16, 128), 0)
    block = jnp.zeros((16, 128), F32)
    for i in range(tokens // 128):
        block = jnp.where(rows == i, idf[:, i * 128 : (i + 1) * 128], block)
    kv[2 * tokens : 2 * tokens + 16] = block.astype(BF16)
    rim[:, features : features + 128] = jnp.broadcast_to(
        idf[:, tokens - 128 : tokens], (16, 128)
    ).astype(BF16)
    for move in moves[1:]:
        move.wait()


def keys_body(k, beta, decay, ids, t_out, uk_out, kend_out, m_out, rows_out, cols_out, eight, a_s, t_s, id_s, sems):
    tokens = k.shape[1]
    heads = beta.shape[0]
    half = tokens // 2
    names = pltpu.make_async_copy(ids, id_s, sems.at[0])
    names.start()
    lane = lax.broadcasted_iota(jnp.int32, (tokens, 128), 1)
    packed = jnp.zeros((tokens, 128), F32)
    for h in range(heads):
        kf = k[0, :, head_lanes(h)].astype(F32)
        norm = lax.rsqrt(jnp.sum(kf * kf, axis=1, keepdims=True) + EPSILON)
        packed = jnp.where(lane == h, norm, packed)
    r8 = packed.T[0:8]
    names.wait()
    idf = id_s[...].astype(F32)
    eight[...] = jnp.zeros_like(eight)
    for h in range(heads):
        eight[0, h : h + 1] = decay[h]
        eight[1, h : h + 1] = beta[h]
    row_index = lax.broadcasted_iota(jnp.int32, (tokens, tokens), 0)
    col_index = lax.broadcasted_iota(jnp.int32, (tokens, tokens), 1)
    upto = jnp.where(row_index <= col_index, 1.0, 0.0)
    run8 = nn(eight[0], upto, lax.Precision.HIGHEST)
    br8 = eight[1] * r8
    fs8 = jnp.where(idf == idf[:, 0:1], jnp.exp(run8), 0.0)
    wend8 = (
        jnp.where(
            idf == idf[:, tokens - 1 : tokens],
            jnp.exp(run8[:, tokens - 1 : tokens] - run8),
            0.0,
        )
        * br8
    )
    ids8 = jnp.broadcast_to(idf, (8, tokens))
    rows_out[...] = jnp.concatenate([run8, br8, ids8], axis=0)
    stacked = jnp.concatenate(
        [run8, wend8, fs8 * r8, fs8, ids8, r8, jnp.zeros((80, tokens), F32)], axis=0
    )
    cols = stacked.T
    cols_out[...] = cols
    visible = (col_index < row_index) & (cols[:, 32:33] == idf)
    for h in range(heads):
        kh = k[0, :, head_lanes(h)]
        kk = nt(kh, kh)
        between = jnp.where(visible, jnp.exp(cols[:, h : h + 1] - run8[h : h + 1]), 0.0)
        a = between * br8[h : h + 1] * (cols[:, 40 + h : 41 + h] * kk)
        a_s[h] = a.astype(BF16)
    ri = lax.broadcasted_iota(jnp.int32, (half, half), 0)
    ci = lax.broadcasted_iota(jnp.int32, (half, half), 1)
    eye = jnp.where(ri == ci, 1.0, 0.0)

    def level_mask(k_bits):
        rb, cb = ri >> k_bits, ci >> k_bits
        return jnp.where(((rb & 1) == 1) & (cb == rb - 1), 1.0, 0.0)

    def diag(h, b):
        return a_s[h, b * half : (b + 1) * half, b * half : (b + 1) * half]

    first = level_mask(0)
    for h in range(heads):
        for b in range(2):
            t_s[2 * h + b] = eye - diag(h, b).astype(F32) * first
    for bits in range(1, (half - 1).bit_length()):
        mask = level_mask(bits).astype(BF16)
        for h in range(heads):
            for b in range(2):
                t = t_s[2 * h + b]
                tb = t.astype(BF16)
                p = nn(diag(h, b) * mask, tb)
                t_s[2 * h + b] = t - nn(tb, p.astype(BF16))
    for h in range(heads):
        t11 = t_s[2 * h].astype(BF16)
        t22 = t_s[2 * h + 1].astype(BF16)
        p = nn(a_s[h, half:tokens, 0:half], t11)
        t_out[h, 0:half, 0:half] = t11
        t_out[h, half:tokens, half:tokens] = t22
        t_out[h, 0:half, half:tokens] = jnp.zeros((half, half), BF16)
        t_out[h, half:tokens, 0:half] = (-nn(t22, p.astype(BF16))).astype(BF16)
    er = lax.broadcasted_iota(jnp.int32, (HEAD, HEAD), 0)
    ec = lax.broadcasted_iota(jnp.int32, (HEAD, HEAD), 1)
    for h in range(heads):
        kf = k[0, :, head_lanes(h)].astype(F32)
        uk = nn(t_out[h], (cols[:, 16 + h : 17 + h] * kf).astype(BF16)).astype(BF16)
        uk_out[h] = uk
        kend = (cols[:, 8 + h : 9 + h] * kf).astype(BF16)
        kend_out[h] = kend
        scale = fs8[h : h + 1, tokens - 1 : tokens]
        m_out[h] = jnp.where(er == ec, scale, 0.0) - tn(uk, kend)


def values_body(v, rim, taps, rows, t, kend, m, after, afters, mi_out, uv_out, x_s, tap_s):
    tokens = v.shape[1]
    features = v.shape[2]
    heads = taps.shape[1]
    count = taps.shape[2]
    first = lax.axis_index("ctx") == 0
    idf = rows[16:17]
    before = rim[0:1, features : features + 128].astype(F32)
    before = jnp.where(first, -1.0, before)
    longer = jnp.concatenate([before, idf], axis=1)
    keeps = [
        (pltpu.roll(longer, j, 1)[:, 128:] == idf).astype(F32) if j else jnp.ones_like(idf)
        for j in range(count)
    ]
    keep = jnp.concatenate(keeps, axis=0)
    tap_s[...] = jnp.zeros_like(tap_s)
    for h in range(heads):
        tap_s[8 * h : 8 * h + count] = taps[0, h] * keep
    cols = tap_s[...].T
    x_s[0:8] = rim[:, 0:features].astype(F32)[8:16]
    x_s[8 : 8 + tokens] = v[0].astype(F32)
    joined = jnp.where(before[0:1, 127:128] == idf[:, 0:1], 1.0, 0.0)
    for h in range(heads):
        conv = cols[:, 8 * h : 8 * h + 1] * x_s[8 : 8 + tokens, head_lanes(h)]
        for j in range(1, count):
            conv = conv + cols[:, 8 * h + j : 8 * h + j + 1] * x_s[8 - j : 8 - j + tokens, head_lanes(h)]
        values = conv / (1.0 + jnp.exp(-conv))
        uv = nn(t[h], values.astype(BF16)).astype(BF16)
        uv_out[h] = uv
        mi_out[h] = (joined * m[h]).astype(BF16)
        mi_out[heads + h] = tn(uv, kend[h]).astype(BF16)


def queries_body(q, k, rim, rows, cols_in, uk, uv, lw, local_out, reader_out, lw_out, lw_s):
    tokens = q.shape[1]
    features = q.shape[2]
    heads = uk.shape[0]
    first = lax.axis_index("ctx") == 0
    idf = rows[16:17]
    before = jnp.where(first, -1.0, rim[0:1, features : features + 128].astype(F32))
    joined = jnp.where(before[0:1, 127:128] == idf[:, 0:1], 1.0, 0.0)
    row_index = lax.broadcasted_iota(jnp.int32, (tokens, tokens), 0)
    col_index = lax.broadcasted_iota(jnp.int32, (tokens, tokens), 1)
    cols = cols_in[...]
    visible = (col_index <= row_index) & (cols[:, 32:33] == idf)
    lw_s[...] = jnp.zeros_like(lw_s)
    for h in range(heads):
        lw_s[h : h + 1] = lw[h]
    lw_out[...] = lw_s[...].T
    for h in range(heads):
        qh = q[0, :, head_lanes(h)]
        qf = qh.astype(F32)
        norm = lax.rsqrt(jnp.sum(qf * qf, axis=1, keepdims=True) + EPSILON)
        qk = nt(qh, k[0, :, head_lanes(h)])
        between = jnp.where(visible, jnp.exp(cols[:, h : h + 1] - rows[h : h + 1]), 0.0)
        reading = (between * rows[8 + h : 9 + h] * (norm * qk)).astype(BF16)
        local_out[h] = nn(reading, uv[h])
        carried = nn(reading, uk[h])
        reader = (cols[:, 24 + h : 25 + h] * norm) * qf - carried
        reader_out[h] = (joined * reader).astype(BF16)


def teacher_body(first_head, last_head, q, cols_in, own, r2, r4, x0, x2, x4, *refs):
    out, full, k_s, v_s, id_s, bias_s = refs[-6:]
    if first_head:
        out[0, :, 0 : first_head * HEAD] = refs[0][0, :, 0 : first_head * HEAD]
    tokens = q.shape[1]
    halves = tokens // 128
    index = lax.axis_index("ctx")
    odd = lax.rem(index, 2) == 1
    def place(slot, source):
        k_s[slot * tokens : (slot + 1) * tokens] = source[0:tokens]
        v_s[slot * tokens : (slot + 1) * tokens] = source[tokens : 2 * tokens]
        behind = 4 - slot
        valid = index >= behind
        names = source[2 * tokens : 2 * tokens + 16].astype(F32)
        for i in range(halves):
            at = (slot * halves + i) * 128
            id_s[:, at : at + 128] = jnp.where(valid, names[i : i + 1], -1.0)

    place(0, r4)
    place(2, r2)
    place(4, own)

    @pl.when(odd)
    def _():
        place(1, x2)
        place(3, x0)

    @pl.when(jnp.logical_not(odd))
    def _():
        place(1, x4)
        place(3, x2)

    width = 5 * tokens
    id_col = cols_in[:, 32:33]
    same = id_col == id_s[...]
    row_index = lax.broadcasted_iota(jnp.int32, (tokens, width), 0)
    col_index = lax.broadcasted_iota(jnp.int32, (tokens, width), 1) - 4 * tokens
    bias_s[...] = jnp.where(same & (col_index <= row_index), 0.0, MASKED)
    scale = math.log2(math.e) / math.sqrt(HEAD)
    span = width - (halves - 1) * 128
    for h in range(first_head, last_head):
        at = head_lanes(h - first_head)
        for r in range(halves):
            rows = slice(r * 128, (r + 1) * 128)
            cols = slice(r * 128, r * 128 + span)
            s = nt(q[0, rows, head_lanes(h)], k_s[cols])
            s = s * scale + bias_s[rows, cols]
            largest = jnp.max(s, axis=1, keepdims=True)
            w = jnp.exp2(s - largest)
            total = jnp.sum(w, axis=1, keepdims=True)
            o = nn(w.astype(BF16), v_s[cols]) / total
            full[rows, at] = o
            out[0, rows, head_lanes(h)] = o.astype(BF16)


def is_odd():
    return lax.rem(lax.axis_index("ctx"), 2) == 1


def chip_body(own, other, after, arrived, m_out, i_out):
    heads, rows, _ = i_out.shape
    odd = is_odd()
    for h in range(heads):
        later_m = jnp.where(odd, own[h], other[h])
        early_m = jnp.where(odd, other[h], own[h])
        later_i = jnp.where(odd, own[heads + h, rows:], other[heads + h, 0:rows])
        early_i = jnp.where(odd, other[heads + h, rows:], own[heads + h, 0:rows])
        m_out[h] = nn(early_m, later_m).astype(BF16)
        i_out[h] = (nn(early_i, later_m) + later_i.astype(F32)).astype(BF16)


def join_body(m, i, arriving, after, out):
    for h in range(m.shape[0]):
        out[h] = (nn(arriving[h], m[h]) + i[h].astype(F32)).astype(BF16)


def finish_body(mine, theirs, other, local, reader, gain, teacher_a, teacher_b, lw, out, sums):
    heads = mine.shape[0]
    odd = is_odd()
    split = teacher_a.shape[1] // HEAD
    total = jnp.zeros(lw.shape, F32)
    for h in range(heads):
        a, b = mine[h], theirs[h]
        s = jnp.concatenate([jnp.where(odd, b, a), jnp.where(odd, a, b)], axis=0)
        stepped = (nn(s, other[h]) + other[heads + h].astype(F32)).astype(BF16)
        s = jnp.where(odd, stepped, s)
        o = local[h] + nt(reader[h], s)
        mean = jnp.sum(o * o, axis=1, keepdims=True) * (1.0 / HEAD)
        student = o * lax.rsqrt(mean + EPSILON) * gain[:, head_lanes(h)]
        out[0, :, head_lanes(h)] = student.astype(BF16)
        teacher = teacher_a[:, head_lanes(h)] if h < split else teacher_b[:, head_lanes(h - split)]
        difference = student - teacher
        total = total + lw[:, h : h + 1] * (difference * difference)
    partial = jnp.sum(jnp.sum(total, axis=0, keepdims=True), axis=1, keepdims=True)
    sums[...] = jnp.broadcast_to(partial, sums.shape)


def on_device(
    student_q,
    student_k,
    student_v,
    beta,
    log_decay,
    kernel,
    out_gain,
    teacher_q,
    teacher_k,
    teacher_v,
    segment_ids,
    loss_weight,
):
    _, tokens, features = student_q.shape
    heads = beta.shape[1]
    shards = lax.axis_size("ctx")
    everyone = shards * lax.axis_size("head") * lax.axis_size("dp")

    def rotated(block, distance):
        return lax.ppermute(block, "ctx", [(i, (i + distance) % shards) for i in range(shards)])

    def swapped(block):
        return lax.ppermute(block, "ctx", [(i, i ^ 1) for i in range(shards)])

    def by_head(block):
        return block.reshape(heads, 1, tokens)

    def crossed(block):
        route = [(i, ((i + 2) % shards) ^ 1) for i in range(shards)]
        return lax.ppermute(block, "ctx", route)

    kv, rim = call(
        pack_body,
        [((2 * tokens + 16, HEAD), BF16), ((16, features + 128), BF16)],
        teacher_k,
        teacher_v,
        student_v,
        segment_ids,
        scratch=[((1, tokens), jnp.int32)],
        hbm=(0, 1, 2, 3),
        vmem=PACK_VMEM,
    )
    rim = rotated(rim, 1)
    r2 = rotated(kv, 2)
    x0 = swapped(kv)
    t, uk, kend, m0, rows, cols = call(
        keys_body,
        [
            ((heads, tokens, tokens), BF16),
            ((heads, tokens, HEAD), BF16),
            ((heads, tokens, HEAD), BF16),
            ((heads, HEAD, HEAD), F32),
            ((24, tokens), F32),
            ((tokens, 128), F32),
        ],
        student_k,
        by_head(beta),
        by_head(log_decay),
        segment_ids,
        scratch=[
            ((2, 8, tokens), F32),
            ((heads, tokens, tokens), BF16),
            ((2 * heads, tokens // 2, tokens // 2), F32),
            ((1, tokens), jnp.int32),
        ],
        hbm=(3,),
        flops=5 * 10**8,
    )
    r4 = rotated(kv, 4)
    mi, uv = call(
        values_body,
        [((2 * heads, HEAD, HEAD), BF16), ((heads, tokens, HEAD), BF16)],
        student_v,
        rim,
        kernel,
        rows,
        t,
        kend,
        m0,
        r2,
        r4,
        scratch=[((8 + tokens, features), F32), ((128, tokens), F32)],
        flops=2 * 10**8,
    )
    mi_other = swapped(mi)
    x2 = swapped(r2)
    local, reader, lw = call(
        queries_body,
        [
            ((heads, tokens, HEAD), F32),
            ((heads, tokens, HEAD), BF16),
            ((tokens, 128), F32),
        ],
        student_q,
        student_k,
        rim,
        rows,
        cols,
        uk,
        uv,
        by_head(loss_weight),
        scratch=[((128, tokens), F32)],
        flops=2 * 10**8,
    )
    m_chip, i_chip = call(
        chip_body,
        [((heads, HEAD, HEAD), BF16), ((heads, HEAD // 2, HEAD), BF16)],
        mi,
        mi_other,
        lw,
        r4,
    )
    behind = rotated(i_chip, 2)
    x4 = swapped(r4)

    def attend(first_head, last_head, *earlier):
        count = last_head - first_head
        return call(
            functools.partial(teacher_body, first_head, last_head),
            [((1, tokens, features), BF16), ((tokens, count * HEAD), F32)],
            teacher_q,
            cols,
            kv,
            r2,
            r4,
            x0,
            x2,
            x4,
            *earlier,
            flops=count * 10**8,
            scratch=[
                ((5 * tokens, HEAD), BF16),
                ((5 * tokens, HEAD), BF16),
                ((1, 5 * tokens), F32),
                ((tokens, 5 * tokens), F32),
            ],
        )

    teacher_out, teacher_a = attend(0, 3)
    (joined,) = call(
        join_body, [((heads, HEAD // 2, HEAD), BF16)], m_chip, i_chip, behind, teacher_a
    )
    mine = rotated(joined, 2)
    theirs = crossed(joined)
    teacher_out, teacher_b = attend(3, heads, teacher_out)
    student_out, sums = call(
        finish_body,
        [((1, tokens, features), BF16), ((everyone, 128), F32)],
        mine,
        theirs,
        mi_other,
        local,
        reader,
        out_gain.reshape(1, features),
        teacher_a,
        teacher_b,
        lw,
    )
    gathered = lax.all_to_all(sums, ("ctx", "head", "dp"), 0, 0, tiled=True)
    loss = jnp.sum(gathered[:, 0]) / (everyone * heads * tokens * HEAD)
    return (student_out, teacher_out, loss)


def solution(mesh):
    placed = (
        P("dp", "ctx", "head"),
        P("dp", "ctx", "head"),
        P("dp", "ctx", "head"),
        P("dp", "head", "ctx"),
        P("dp", "head", "ctx"),
        P("dp", "head", None, "ctx"),
        P("head"),
        P("dp", "ctx", "head"),
        P("dp", "ctx", "head"),
        P("dp", "ctx", "head"),
        P("dp", "ctx"),
        P("dp", "head", "ctx"),
    )
    return jax.shard_map(
        on_device,
        mesh=mesh,
        in_specs=placed,
        out_specs=(P("dp", "ctx", "head"), P("dp", "ctx", "head"), P()),
        check_vma=False,
    )
```

```python
import functools
import math

import jax
import jax.numpy as jnp
from jax import lax
from jax.experimental import pallas as pl
from jax.experimental.pallas import tpu as pltpu
from jax.sharding import PartitionSpec as P

EPSILON = 1e-06
MASKED = -1e30
HEAD = 128
F32 = jnp.float32
BF16 = jnp.bfloat16
VMEM_BYTES = 32 * 1024 * 1024
PACK_VMEM = 62 * 1024 * 1024


def nn(a, b, precision=None):
    return lax.dot_general(
        a, b, (((1,), (0,)), ((), ())), precision=precision, preferred_element_type=F32
    )


def nt(a, b):
    return lax.dot_general(a, b, (((1,), (1,)), ((), ())), preferred_element_type=F32)


def tn(a, b):
    return lax.dot_general(a, b, (((0,), (0,)), ((), ())), preferred_element_type=F32)


def head_lanes(h):
    return slice(h * HEAD, (h + 1) * HEAD)


def call(body, outs, *args, scratch=(), hbm=(), hbm_out=(), copies=0, flops=0, vmem=VMEM_BYTES):
    buffers = [pltpu.VMEM(s, d) for s, d in scratch]
    copies = copies or len(hbm)
    if copies:
        buffers.append(pltpu.SemaphoreType.DMA((copies,)))
    return pl.pallas_call(
        body,
        out_shape=[jax.ShapeDtypeStruct(s, d) for s, d in outs],
        in_specs=[
            pl.BlockSpec(memory_space=pltpu.HBM if i in hbm else pltpu.VMEM)
            for i in range(len(args))
        ],
        out_specs=[
            pl.BlockSpec(memory_space=pltpu.HBM if i in hbm_out else pltpu.VMEM)
            for i in range(len(outs))
        ],
        scratch_shapes=buffers,
        compiler_params=pltpu.CompilerParams(vmem_limit_bytes=vmem),
        cost_estimate=pl.CostEstimate(flops=flops, bytes_accessed=0, transcendentals=0),
    )(*args)


def pack_body(tk, tv, sv, ids, kv, rim, id_s, sems):
    tokens = tk.shape[1]
    features = sv.shape[2]
    moves = [
        pltpu.make_async_copy(ids, id_s, sems.at[0]),
        pltpu.make_async_copy(
            sv.at[0, tokens - 16 : tokens, :], rim.at[:, 0:features], sems.at[1]
        ),
        pltpu.make_async_copy(tk.at[0], kv.at[0:tokens], sems.at[2]),
        pltpu.make_async_copy(tv.at[0], kv.at[tokens : 2 * tokens], sems.at[3]),
    ]
    for move in moves:
        move.start()
    moves[0].wait()
    idf = id_s[...].astype(F32)
    rows = lax.broadcasted_iota(jnp.int32, (16, 128), 0)
    block = jnp.zeros((16, 128), F32)
    for i in range(tokens // 128):
        block = jnp.where(rows == i, idf[:, i * 128 : (i + 1) * 128], block)
    kv[2 * tokens : 2 * tokens + 16] = block.astype(BF16)
    rim[:, features : features + 128] = jnp.broadcast_to(
        idf[:, tokens - 128 : tokens], (16, 128)
    ).astype(BF16)
    for move in moves[1:]:
        move.wait()


def eye(n):
    rows = lax.broadcasted_iota(jnp.int32, (n, n), 0)
    cols = lax.broadcasted_iota(jnp.int32, (n, n), 1)
    return jnp.where(rows == cols, 1.0, 0.0)


def keys_body(k, beta, decay, ids, t_out, uk_out, m_out, rows_out, cols_out, eight, a_s, c_s, t_s, beta_s, decay_s, id_s, sems):
    tokens = k.shape[1]
    heads = beta.shape[0]
    half = tokens // 2
    small = c_s.shape[1]
    moves = [
        pltpu.make_async_copy(source, target, sems.at[i])
        for i, (source, target) in enumerate(((beta, beta_s), (decay, decay_s), (ids, id_s)))
    ]
    for move in moves:
        move.start()
    lane = lax.broadcasted_iota(jnp.int32, (tokens, 128), 1)
    packed = jnp.zeros((tokens, 128), F32)
    for h in range(heads):
        kf = k[0, :, head_lanes(h)].astype(F32)
        norm = lax.rsqrt(jnp.sum(kf * kf, axis=1, keepdims=True) + EPSILON)
        packed = jnp.where(lane == h, norm, packed)
    r8 = packed.T[0:8]
    for move in moves:
        move.wait()
    idf = id_s[...].astype(F32)
    eight[...] = jnp.zeros_like(eight)
    for h in range(heads):
        eight[0, h : h + 1] = decay_s[h]
        eight[1, h : h + 1] = beta_s[h]
    row_index = lax.broadcasted_iota(jnp.int32, (tokens, tokens), 0)
    col_index = lax.broadcasted_iota(jnp.int32, (tokens, tokens), 1)
    upto = jnp.where(row_index <= col_index, 1.0, 0.0)
    run8 = nn(eight[0], upto, lax.Precision.HIGHEST)
    br8 = eight[1] * r8
    fs8 = jnp.where(idf == idf[:, 0:1], jnp.exp(run8), 0.0)
    fsr8 = fs8 * r8
    wend8 = (
        jnp.where(
            idf == idf[:, tokens - 1 : tokens],
            jnp.exp(run8[:, tokens - 1 : tokens] - run8),
            0.0,
        )
        * br8
    )
    ids8 = jnp.broadcast_to(idf, (8, tokens))
    rows_out[...] = jnp.concatenate([run8, br8, ids8, wend8], axis=0)
    stacked = jnp.concatenate([run8, r8, fs8, ids8, jnp.zeros((96, tokens), F32)], axis=0)
    cols = stacked.T
    cols_out[...] = cols

    rh = lax.broadcasted_iota(jnp.int32, (half, half), 0)
    ch = lax.broadcasted_iota(jnp.int32, (half, half), 1)
    below = ch < rh
    cl = lax.broadcasted_iota(jnp.int32, (small, half), 1)
    owns = [(cl // small) == i for i in range(half // small)]
    for h in range(heads):
        kh = k[0, :, head_lanes(h)]
        for at, (i, j) in enumerate(((0, 0), (1, 0), (1, 1))):
            ri, rj = slice(i * half, (i + 1) * half), slice(j * half, (j + 1) * half)
            kk = nt(kh[ri], kh[rj])
            seen = cols[ri, 24:25] == idf[:, rj]
            if i == j:
                seen = seen & below
            between = jnp.where(seen, jnp.exp(cols[ri, h : h + 1] - run8[h : h + 1, rj]), 0.0)
            a = between * br8[h : h + 1, rj] * (cols[ri, 8 + h : 9 + h] * kk)
            a_s[h, at] = a.astype(BF16)
            if i == j:
                c = jnp.zeros((small, half), F32)
                for n, own in enumerate(owns):
                    c = jnp.where(own, a[n * small : (n + 1) * small], c)
                c_s[2 * h + i] = c

    rs = lax.broadcasted_iota(jnp.int32, (small, half), 0)
    cs = cl % small
    blocks = [(h, b) for h in range(heads) for b in range(2)]
    inside = jnp.where((rh // small) == (ch // small), 1.0, 0.0)
    inside16 = inside.astype(BF16)

    def merges(r, c, bits):
        rb, cb = r >> bits, c >> bits
        return jnp.where(((rb & 1) == 1) & (cb == rb - 1), 1.0, 0.0)

    def spread(x):
        return jnp.concatenate([x] * (half // small), axis=0) * inside16

    unit = jnp.where(rs == cs, 1.0, 0.0)
    first = merges(rs, cs, 0)
    ts = [unit - c_s[n] * first for n in range(len(blocks))]
    for bits in range(1, (small - 1).bit_length()):
        mask = merges(rs, cs, bits)
        tb = [t.astype(BF16) for t in ts]
        ps = [nn((c_s[n] * mask).astype(BF16), spread(tb[n])) for n in range(len(blocks))]
        ts = [t - nn(tb[n], spread(ps[n].astype(BF16))) for n, t in enumerate(ts)]
    for n, t in enumerate(ts):
        t_s[n] = jnp.concatenate([t] * (half // small), axis=0) * inside
    for bits in range((small - 1).bit_length(), (half - 1).bit_length()):
        size = 1 << bits
        odd = [slice(i * size, (i + 1) * size) for i in range(1, half // size, 2)]
        mask = merges(rh, ch, bits).astype(BF16)
        tb = [t_s[n].astype(BF16) for n in range(len(blocks))]
        ps = [
            nn(jnp.concatenate([(a_s[h, 2 * b, r] * mask[r]) for r in odd], axis=0), tb[n])
            for n, (h, b) in enumerate(blocks)
        ]
        changes = []
        for n in range(len(blocks)):
            p = ps[n].astype(BF16)
            pieces = []
            for i in range(len(odd)):
                pieces += [jnp.zeros((size, half), BF16), p[i * size : (i + 1) * size]]
            changes.append(
                nn(
                    jnp.concatenate([tb[n][r] for r in odd], axis=0),
                    jnp.concatenate(pieces, axis=0),
                )
            )
        for n in range(len(blocks)):
            for i, r in enumerate(odd):
                t_s[n, r] = t_s[n, r] - changes[n][i * size : (i + 1) * size]
    tb = [t_s[n].astype(BF16) for n in range(len(blocks))]
    one = eye(HEAD)
    one16 = one.astype(BF16)
    keys = [k[0, :, head_lanes(h)] for h in range(heads)]
    xs = [nt(one16, keys[h]) for h in range(heads)]
    ps = [nn(a_s[h, 1], tb[2 * h]).astype(BF16) for h in range(heads)]
    t21 = [(-nn(tb[2 * h + 1], ps[h])).astype(BF16) for h in range(heads)]
    for h in range(heads):
        t_out[h, 0:half, 0:half] = tb[2 * h]
        t_out[h, half:tokens, half:tokens] = tb[2 * h + 1]
        t_out[h, 0:half, half:tokens] = jnp.zeros((half, half), BF16)
        t_out[h, half:tokens, 0:half] = t21[h]
    none = jnp.zeros((half, half), BF16)
    ts = [
        jnp.concatenate(
            [
                jnp.concatenate([tb[2 * h], none], axis=1),
                jnp.concatenate([t21[h], tb[2 * h + 1]], axis=1),
            ],
            axis=0,
        )
        for h in range(heads)
    ]
    uks = [nt((xs[h] * fsr8[h : h + 1]).astype(BF16), ts[h]) for h in range(heads)]
    ms = [nn((uks[h] * wend8[h : h + 1]).astype(BF16), keys[h]) for h in range(heads)]
    for h in range(heads):
        uk_out[h] = uks[h].astype(BF16)
        m_out[h] = one * fs8[h : h + 1, tokens - 1 : tokens] - ms[h]


def values_body(v, rim, taps, rows, t, k, m, after, mi_out, uv_out):
    features = v.shape[2]
    heads = taps.shape[1]
    count = taps.shape[2]
    first = lax.axis_index("ctx") == 0
    idf = rows[16:17]
    before = rim[0:1, features : features + 128].astype(F32)
    before = jnp.where(first, -1.0, before)
    longer = jnp.concatenate([before, idf], axis=1)
    keep = [
        jnp.where(pltpu.roll(longer, j, 1)[:, 128:] == idf, 1.0, 0.0) for j in range(1, count)
    ]
    joined = jnp.where(before[0:1, 127:128] == idf[:, 0:1], 1.0, 0.0)
    one16 = eye(HEAD).astype(BF16)
    empty = jnp.zeros((112, HEAD), BF16)
    every = range(heads)
    keys = [k[0, :, head_lanes(h)] for h in every]
    owns = [nt(one16, v[0, :, head_lanes(h)]) for h in every]
    rims = [nt(one16, jnp.concatenate([empty, rim[:, head_lanes(h)]], axis=0)) for h in every]
    values = []
    for h in every:
        whole = jnp.concatenate([rims[h], owns[h]], axis=1)
        conv = taps[0, h, 0:1] * owns[h]
        for j in range(1, count):
            conv = conv + (taps[0, h, j : j + 1] * keep[j - 1]) * pltpu.roll(whole, j, 1)[:, 128:]
        values.append((conv / (1.0 + jnp.exp(-conv))).astype(BF16))
    uvs = [nt(values[h], t[h]) for h in every]
    ends = [nn((uvs[h] * rows[24 + h : 25 + h]).astype(BF16), keys[h]) for h in every]
    for h in every:
        uv_out[h] = uvs[h].astype(BF16)
        mi_out[h] = (joined * m[h]).astype(BF16)
        mi_out[heads + h] = ends[h].astype(BF16)


def queries_body(q, k, rim, rows, cols_in, uk, uv, lw, local_out, reader_out, lw_out, lw_s):
    tokens = q.shape[1]
    features = q.shape[2]
    heads = uk.shape[0]
    first = lax.axis_index("ctx") == 0
    idf = rows[16:17]
    before = jnp.where(first, -1.0, rim[0:1, features : features + 128].astype(F32))
    joined = jnp.where(before[0:1, 127:128] == idf[:, 0:1], 1.0, 0.0)
    row_index = lax.broadcasted_iota(jnp.int32, (tokens, tokens), 0)
    col_index = lax.broadcasted_iota(jnp.int32, (tokens, tokens), 1)
    cols = cols_in[...]
    visible = (col_index <= row_index) & (cols[:, 24:25] == idf)
    lw_s[...] = jnp.zeros_like(lw_s)
    for h in range(heads):
        lw_s[h : h + 1] = lw[h]
    lw_out[...] = lw_s[...].T
    every = range(heads)
    qs = [q[0, :, head_lanes(h)] for h in every]
    qks = [nt(qs[h], k[0, :, head_lanes(h)]) for h in every]
    norms, readings = [], []
    for h in every:
        qf = qs[h].astype(F32)
        norms.append(lax.rsqrt(jnp.sum(qf * qf, axis=1, keepdims=True) + EPSILON))
        between = jnp.where(visible, jnp.exp(cols[:, h : h + 1] - rows[h : h + 1]), 0.0)
        readings.append((between * rows[8 + h : 9 + h] * (norms[h] * qks[h])).astype(BF16))
    both = [nt(readings[h], jnp.concatenate([uv[h], uk[h]], axis=0)) for h in every]
    for h in every:
        local_out[h] = both[h][:, 0:HEAD]
        reader = (cols[:, 16 + h : 17 + h] * norms[h]) * qs[h].astype(F32) - both[h][:, HEAD:]
        reader_out[h] = (joined * reader).astype(BF16)


def teacher_body(first_head, last_head, q, cols_in, own, r2, r4, x0, x2, x4, *refs):
    out, full, k_s, v_s, id_s, bias_s = refs[-6:]
    if first_head:
        out[0, :, 0 : first_head * HEAD] = refs[0][0, :, 0 : first_head * HEAD]
    tokens = q.shape[1]
    halves = tokens // 128
    index = lax.axis_index("ctx")
    odd = lax.rem(index, 2) == 1
    def place(slot, source):
        k_s[slot * tokens : (slot + 1) * tokens] = source[0:tokens]
        v_s[slot * tokens : (slot + 1) * tokens] = source[tokens : 2 * tokens]
        behind = 4 - slot
        valid = index >= behind
        names = source[2 * tokens : 2 * tokens + 16].astype(F32)
        for i in range(halves):
            at = (slot * halves + i) * 128
            id_s[:, at : at + 128] = jnp.where(valid, names[i : i + 1], -1.0)

    place(0, r4)
    place(2, r2)
    place(4, own)

    @pl.when(odd)
    def _():
        place(1, x2)
        place(3, x0)

    @pl.when(jnp.logical_not(odd))
    def _():
        place(1, x4)
        place(3, x2)

    width = 5 * tokens
    id_col = cols_in[:, 24:25]
    same = id_col == id_s[...]
    row_index = lax.broadcasted_iota(jnp.int32, (tokens, width), 0)
    col_index = lax.broadcasted_iota(jnp.int32, (tokens, width), 1) - 4 * tokens
    bias_s[...] = jnp.where(same & (col_index <= row_index), 0.0, MASKED)
    scale = math.log2(math.e) / math.sqrt(HEAD)
    span = width - (halves - 1) * 128
    tiles = [(h, r) for h in range(first_head, last_head) for r in range(halves)]

    def scores(h, r):
        return nt(q[0, r * 128 : (r + 1) * 128, head_lanes(h)], k_s[r * 128 : r * 128 + span])

    ahead = 2
    ss = [scores(*tile) for tile in tiles[:ahead]]
    for n, (h, r) in enumerate(tiles):
        if n + ahead < len(tiles):
            ss.append(scores(*tiles[n + ahead]))
        at = head_lanes(h - first_head)
        rows = slice(r * 128, (r + 1) * 128)
        cols = slice(r * 128, r * 128 + span)
        s = ss[n] * scale + bias_s[rows, cols]
        largest = jnp.max(s, axis=1, keepdims=True)
        w = jnp.exp2(s - largest)
        total = jnp.sum(w, axis=1, keepdims=True)
        o = nn(w.astype(BF16), v_s[cols]) / total
        full[rows, at] = o
        out[0, rows, head_lanes(h)] = o.astype(BF16)


def is_odd():
    return lax.rem(lax.axis_index("ctx"), 2) == 1


def chip_body(own, other, m_out, i_out):
    heads, rows, _ = i_out.shape
    every = range(heads)
    odd = is_odd()
    later_m = [jnp.where(odd, own[h], other[h]) for h in every]
    early_m = [jnp.where(odd, other[h], own[h]) for h in every]
    early_i = [jnp.where(odd, other[heads + h, rows:], own[heads + h, 0:rows]) for h in every]
    ms = [nn(early_m[h], later_m[h]) for h in every]
    ends = [nn(early_i[h], later_m[h]) for h in every]
    for h in every:
        later_i = jnp.where(odd, own[heads + h, rows:], other[heads + h, 0:rows])
        m_out[h] = ms[h].astype(BF16)
        i_out[h] = (ends[h] + later_i.astype(F32)).astype(BF16)


def join_body(m, i, arriving, after, out):
    every = range(m.shape[0])
    ends = [nn(arriving[h], m[h]) for h in every]
    for h in every:
        out[h] = (ends[h] + i[h].astype(F32)).astype(BF16)


def finish_body(mine, theirs, other, local, reader, gain, teachers, lw, out, sums):
    heads = mine.shape[0]
    every = range(heads)
    odd = is_odd()
    total = jnp.zeros(lw.shape, F32)
    states = []
    for h in every:
        a, b = mine[h], theirs[h]
        states.append(jnp.concatenate([jnp.where(odd, b, a), jnp.where(odd, a, b)], axis=0))
    steps = [nn(states[h], other[h]) for h in every]
    for h in every:
        step = (steps[h] + other[heads + h].astype(F32)).astype(BF16)
        states[h] = jnp.where(odd, step, states[h])
    os = [local[h] + nt(reader[h], states[h]) for h in every]
    for h in every:
        mean = jnp.sum(os[h] * os[h], axis=1, keepdims=True) * (1.0 / HEAD)
        student = os[h] * lax.rsqrt(mean + EPSILON) * gain[:, head_lanes(h)]
        out[0, :, head_lanes(h)] = student.astype(BF16)
        difference = student - teachers[:, head_lanes(h)]
        total = total + lw[:, h : h + 1] * (difference * difference)
    partial = jnp.sum(jnp.sum(total, axis=0, keepdims=True), axis=1, keepdims=True)
    sums[...] = jnp.broadcast_to(partial, sums.shape)


def on_device(
    student_q,
    student_k,
    student_v,
    beta,
    log_decay,
    kernel,
    out_gain,
    teacher_q,
    teacher_k,
    teacher_v,
    segment_ids,
    loss_weight,
):
    _, tokens, features = student_q.shape
    heads = beta.shape[1]
    shards = lax.axis_size("ctx")
    everyone = shards * lax.axis_size("head") * lax.axis_size("dp")

    def rotated(block, distance):
        return lax.ppermute(block, "ctx", [(i, (i + distance) % shards) for i in range(shards)])

    def swapped(block):
        return lax.ppermute(block, "ctx", [(i, i ^ 1) for i in range(shards)])

    def by_head(block):
        return block.reshape(heads, 1, tokens)

    def crossed(block):
        route = [(i, ((i + 2) % shards) ^ 1) for i in range(shards)]
        return lax.ppermute(block, "ctx", route)

    kv, rim = call(
        pack_body,
        [((2 * tokens + 16, HEAD), BF16), ((16, features + 128), BF16)],
        teacher_k,
        teacher_v,
        student_v,
        segment_ids,
        scratch=[((1, tokens), jnp.int32)],
        hbm=(0, 1, 2, 3),
        vmem=PACK_VMEM,
    )
    rim = rotated(rim, 1)
    r2 = rotated(kv, 2)
    x0 = swapped(kv)
    t, uk, m0, rows, cols = call(
        keys_body,
        [
            ((heads, tokens, tokens), BF16),
            ((heads, HEAD, tokens), BF16),
            ((heads, HEAD, HEAD), F32),
            ((32, tokens), F32),
            ((tokens, 128), F32),
        ],
        student_k,
        by_head(beta),
        by_head(log_decay),
        segment_ids,
        scratch=[
            ((2, 8, tokens), F32),
            ((heads, 3, tokens // 2, tokens // 2), BF16),
            ((2 * heads, 32, tokens // 2), F32),
            ((2 * heads, tokens // 2, tokens // 2), F32),
            ((heads, 1, tokens), F32),
            ((heads, 1, tokens), F32),
            ((1, tokens), jnp.int32),
        ],
        hbm=(1, 2, 3),
        flops=5 * 10**8,
    )
    r4 = rotated(r2, 2)
    mi, uv = call(
        values_body,
        [((2 * heads, HEAD, HEAD), BF16), ((heads, HEAD, tokens), BF16)],
        student_v,
        rim,
        kernel,
        rows,
        t,
        student_k,
        m0,
        r2,
        flops=2 * 10**8,
    )
    mi_other = swapped(mi)
    x2 = swapped(r2)
    local, reader, lw = call(
        queries_body,
        [
            ((heads, tokens, HEAD), F32),
            ((heads, tokens, HEAD), BF16),
            ((tokens, 128), F32),
        ],
        student_q,
        student_k,
        rim,
        rows,
        cols,
        uk,
        uv,
        by_head(loss_weight),
        scratch=[((128, tokens), F32)],
        flops=2 * 10**8,
    )
    m_chip, i_chip = call(
        chip_body,
        [((heads, HEAD, HEAD), BF16), ((heads, HEAD // 2, HEAD), BF16)],
        mi,
        mi_other,
    )
    behind = rotated(i_chip, 2)
    x4 = swapped(r4)

    def attend(first_head, last_head, *earlier):
        count = last_head - first_head
        return call(
            functools.partial(teacher_body, first_head, last_head),
            [((1, tokens, features), BF16), ((tokens, count * HEAD), F32)],
            teacher_q,
            cols,
            kv,
            r2,
            r4,
            x0,
            x2,
            x4,
            *earlier,
            flops=count * 10**8,
            scratch=[
                ((5 * tokens, HEAD), BF16),
                ((5 * tokens, HEAD), BF16),
                ((1, 5 * tokens), F32),
                ((tokens, 5 * tokens), F32),
            ],
        )

    (joined,) = call(
        join_body, [((heads, HEAD // 2, HEAD), BF16)], m_chip, i_chip, behind, lw
    )
    mine = rotated(joined, 2)
    theirs = crossed(joined)
    teacher_out, teacher = attend(0, heads)
    student_out, sums = call(
        finish_body,
        [((1, tokens, features), BF16), ((everyone, 128), F32)],
        mine,
        theirs,
        mi_other,
        local,
        reader,
        out_gain.reshape(1, features),
        teacher,
        lw,
    )
    gathered = lax.all_to_all(sums, ("ctx", "head", "dp"), 0, 0, tiled=True)
    loss = jnp.sum(gathered[:, 0]) / (everyone * heads * tokens * HEAD)
    return (student_out, teacher_out, loss)


def solution(mesh):
    placed = (
        P("dp", "ctx", "head"),
        P("dp", "ctx", "head"),
        P("dp", "ctx", "head"),
        P("dp", "head", "ctx"),
        P("dp", "head", "ctx"),
        P("dp", "head", None, "ctx"),
        P("head"),
        P("dp", "ctx", "head"),
        P("dp", "ctx", "head"),
        P("dp", "ctx", "head"),
        P("dp", "ctx"),
        P("dp", "head", "ctx"),
    )
    return jax.shard_map(
        on_device,
        mesh=mesh,
        in_specs=placed,
        out_specs=(P("dp", "ctx", "head"), P("dp", "ctx", "head"), P()),
        check_vma=False,
    )
```

```python
import functools
import math

import jax
import jax.numpy as jnp
from jax import lax
from jax.experimental import pallas as pl
from jax.experimental.pallas import tpu as pltpu
from jax.sharding import PartitionSpec as P

EPSILON = 1e-06
MASKED = -1e30
HEAD = 128
F32 = jnp.float32
BF16 = jnp.bfloat16
VMEM_BYTES = 32 * 1024 * 1024
PACK_VMEM = 62 * 1024 * 1024


def nn(a, b, precision=None):
    return lax.dot_general(
        a, b, (((1,), (0,)), ((), ())), precision=precision, preferred_element_type=F32
    )


def nt(a, b):
    return lax.dot_general(a, b, (((1,), (1,)), ((), ())), preferred_element_type=F32)


def tn(a, b):
    return lax.dot_general(a, b, (((0,), (0,)), ((), ())), preferred_element_type=F32)


def head_lanes(h):
    return slice(h * HEAD, (h + 1) * HEAD)


def call(body, outs, *args, scratch=(), hbm=(), hbm_out=(), copies=0, flops=0, vmem=VMEM_BYTES):
    buffers = [pltpu.VMEM(s, d) for s, d in scratch]
    copies = copies or len(hbm)
    if copies:
        buffers.append(pltpu.SemaphoreType.DMA((copies,)))
    return pl.pallas_call(
        body,
        out_shape=[jax.ShapeDtypeStruct(s, d) for s, d in outs],
        in_specs=[
            pl.BlockSpec(memory_space=pltpu.HBM if i in hbm else pltpu.VMEM)
            for i in range(len(args))
        ],
        out_specs=[
            pl.BlockSpec(memory_space=pltpu.HBM if i in hbm_out else pltpu.VMEM)
            for i in range(len(outs))
        ],
        scratch_shapes=buffers,
        compiler_params=pltpu.CompilerParams(vmem_limit_bytes=vmem),
        cost_estimate=pl.CostEstimate(flops=flops, bytes_accessed=0, transcendentals=0),
    )(*args)


def pack_body(tk, tv, sv, ids, kv, rim, id_s, sems):
    tokens = tk.shape[1]
    features = sv.shape[2]
    moves = [
        pltpu.make_async_copy(ids, id_s, sems.at[0]),
        pltpu.make_async_copy(
            sv.at[0, tokens - 16 : tokens, :], rim.at[:, 0:features], sems.at[1]
        ),
        pltpu.make_async_copy(tk.at[0], kv.at[0:tokens], sems.at[2]),
        pltpu.make_async_copy(tv.at[0], kv.at[tokens : 2 * tokens], sems.at[3]),
    ]
    for move in moves:
        move.start()
    moves[0].wait()
    idf = id_s[...].astype(F32)
    rows = lax.broadcasted_iota(jnp.int32, (16, 128), 0)
    block = jnp.zeros((16, 128), F32)
    for i in range(tokens // 128):
        block = jnp.where(rows == i, idf[:, i * 128 : (i + 1) * 128], block)
    kv[2 * tokens : 2 * tokens + 16] = block.astype(BF16)
    rim[:, features : features + 128] = jnp.broadcast_to(
        idf[:, tokens - 128 : tokens], (16, 128)
    ).astype(BF16)
    for move in moves[1:]:
        move.wait()


def eye(n):
    rows = lax.broadcasted_iota(jnp.int32, (n, n), 0)
    cols = lax.broadcasted_iota(jnp.int32, (n, n), 1)
    return jnp.where(rows == cols, 1.0, 0.0)


def keys_body(k, beta, decay, ids, t_out, uk_out, m_out, rows_out, cols_out, eight, a_s, c_s, t_s, beta_s, decay_s, id_s, sems):
    tokens = k.shape[1]
    heads = beta.shape[0]
    half = tokens // 2
    small = c_s.shape[1]
    moves = [
        pltpu.make_async_copy(source, target, sems.at[i])
        for i, (source, target) in enumerate(((beta, beta_s), (decay, decay_s), (ids, id_s)))
    ]
    for move in moves:
        move.start()
    lane = lax.broadcasted_iota(jnp.int32, (tokens, 128), 1)
    packed = jnp.zeros((tokens, 128), F32)
    for h in range(heads):
        kf = k[0, :, head_lanes(h)].astype(F32)
        norm = lax.rsqrt(jnp.sum(kf * kf, axis=1, keepdims=True) + EPSILON)
        packed = jnp.where(lane == h, norm, packed)
    r8 = packed.T[0:8]
    for move in moves:
        move.wait()
    idf = id_s[...].astype(F32)
    eight[...] = jnp.zeros_like(eight)
    for h in range(heads):
        eight[0, h : h + 1] = decay_s[h]
        eight[1, h : h + 1] = beta_s[h]
    row_index = lax.broadcasted_iota(jnp.int32, (tokens, tokens), 0)
    col_index = lax.broadcasted_iota(jnp.int32, (tokens, tokens), 1)
    upto = jnp.where(row_index <= col_index, 1.0, 0.0)
    run8 = nn(eight[0], upto, lax.Precision.HIGHEST)
    br8 = eight[1] * r8
    fs8 = jnp.where(idf == idf[:, 0:1], jnp.exp(run8), 0.0)
    fsr8 = fs8 * r8
    wend8 = (
        jnp.where(
            idf == idf[:, tokens - 1 : tokens],
            jnp.exp(run8[:, tokens - 1 : tokens] - run8),
            0.0,
        )
        * br8
    )
    ids8 = jnp.broadcast_to(idf, (8, tokens))
    rows_out[...] = jnp.concatenate([run8, br8, ids8, wend8], axis=0)
    stacked = jnp.concatenate([run8, r8, fs8, ids8, jnp.zeros((96, tokens), F32)], axis=0)
    cols = stacked.T
    cols_out[...] = cols

    rh = lax.broadcasted_iota(jnp.int32, (half, half), 0)
    ch = lax.broadcasted_iota(jnp.int32, (half, half), 1)
    below = ch < rh
    cl = lax.broadcasted_iota(jnp.int32, (small, half), 1)
    owns = [(cl // small) == i for i in range(half // small)]
    for h in range(heads):
        kh = k[0, :, head_lanes(h)]
        for at, (i, j) in enumerate(((0, 0), (1, 0), (1, 1))):
            ri, rj = slice(i * half, (i + 1) * half), slice(j * half, (j + 1) * half)
            kk = nt(kh[ri], kh[rj])
            seen = cols[ri, 24:25] == idf[:, rj]
            if i == j:
                seen = seen & below
            between = jnp.where(seen, jnp.exp(cols[ri, h : h + 1] - run8[h : h + 1, rj]), 0.0)
            a = between * br8[h : h + 1, rj] * (cols[ri, 8 + h : 9 + h] * kk)
            a_s[h, at] = a.astype(BF16)
            if i == j:
                c = jnp.zeros((small, half), F32)
                for n, own in enumerate(owns):
                    c = jnp.where(own, a[n * small : (n + 1) * small], c)
                c_s[2 * h + i] = c

    rs = lax.broadcasted_iota(jnp.int32, (small, half), 0)
    cs = cl % small
    blocks = [(h, b) for h in range(heads) for b in range(2)]
    inside = jnp.where((rh // small) == (ch // small), 1.0, 0.0)
    inside16 = inside.astype(BF16)

    def merges(r, c, bits):
        rb, cb = r >> bits, c >> bits
        return jnp.where(((rb & 1) == 1) & (cb == rb - 1), 1.0, 0.0)

    def spread(x):
        return jnp.concatenate([x] * (half // small), axis=0) * inside16

    unit = jnp.where(rs == cs, 1.0, 0.0)
    first = merges(rs, cs, 0)
    ts = [unit - c_s[n] * first for n in range(len(blocks))]
    for bits in range(1, (small - 1).bit_length()):
        mask = merges(rs, cs, bits)
        tb = [t.astype(BF16) for t in ts]
        ps = [nn((c_s[n] * mask).astype(BF16), spread(tb[n])) for n in range(len(blocks))]
        ts = [t - nn(tb[n], spread(ps[n].astype(BF16))) for n, t in enumerate(ts)]
    for n, t in enumerate(ts):
        t_s[n] = jnp.concatenate([t] * (half // small), axis=0) * inside
    for bits in range((small - 1).bit_length(), (half - 1).bit_length()):
        size = 1 << bits
        odd = [slice(i * size, (i + 1) * size) for i in range(1, half // size, 2)]
        mask = merges(rh, ch, bits).astype(BF16)
        tb = [t_s[n].astype(BF16) for n in range(len(blocks))]
        ps = [
            nn(jnp.concatenate([(a_s[h, 2 * b, r] * mask[r]) for r in odd], axis=0), tb[n])
            for n, (h, b) in enumerate(blocks)
        ]
        changes = []
        for n in range(len(blocks)):
            p = ps[n].astype(BF16)
            pieces = []
            for i in range(len(odd)):
                pieces += [jnp.zeros((size, half), BF16), p[i * size : (i + 1) * size]]
            changes.append(
                nn(
                    jnp.concatenate([tb[n][r] for r in odd], axis=0),
                    jnp.concatenate(pieces, axis=0),
                )
            )
        for n in range(len(blocks)):
            for i, r in enumerate(odd):
                t_s[n, r] = t_s[n, r] - changes[n][i * size : (i + 1) * size]
    tb = [t_s[n].astype(BF16) for n in range(len(blocks))]
    one = eye(HEAD)
    one16 = one.astype(BF16)
    keys = [k[0, :, head_lanes(h)] for h in range(heads)]
    xs = [nt(one16, keys[h]) for h in range(heads)]
    ps = [nn(a_s[h, 1], tb[2 * h]).astype(BF16) for h in range(heads)]
    t21 = [(-nn(tb[2 * h + 1], ps[h])).astype(BF16) for h in range(heads)]
    for h in range(heads):
        t_out[h, 0:half, 0:half] = tb[2 * h]
        t_out[h, half:tokens, half:tokens] = tb[2 * h + 1]
        t_out[h, 0:half, half:tokens] = jnp.zeros((half, half), BF16)
        t_out[h, half:tokens, 0:half] = t21[h]
    none = jnp.zeros((half, half), BF16)
    ts = [
        jnp.concatenate(
            [
                jnp.concatenate([tb[2 * h], none], axis=1),
                jnp.concatenate([t21[h], tb[2 * h + 1]], axis=1),
            ],
            axis=0,
        )
        for h in range(heads)
    ]
    uks = [nt((xs[h] * fsr8[h : h + 1]).astype(BF16), ts[h]) for h in range(heads)]
    ms = [nn((uks[h] * wend8[h : h + 1]).astype(BF16), keys[h]) for h in range(heads)]
    for h in range(heads):
        uk_out[h] = uks[h].astype(BF16)
        m_out[h] = one * fs8[h : h + 1, tokens - 1 : tokens] - ms[h]


def values_body(v, rim, taps, rows, t, k, m, after, mi_out, uv_out):
    features = v.shape[2]
    heads = taps.shape[1]
    count = taps.shape[2]
    first = lax.axis_index("ctx") == 0
    idf = rows[16:17]
    before = rim[0:1, features : features + 128].astype(F32)
    before = jnp.where(first, -1.0, before)
    longer = jnp.concatenate([before, idf], axis=1)
    keep = [
        jnp.where(pltpu.roll(longer, j, 1)[:, 128:] == idf, 1.0, 0.0) for j in range(1, count)
    ]
    joined = jnp.where(before[0:1, 127:128] == idf[:, 0:1], 1.0, 0.0)
    one16 = eye(HEAD).astype(BF16)
    empty = jnp.zeros((112, HEAD), BF16)
    every = range(heads)
    keys = [k[0, :, head_lanes(h)] for h in every]
    owns = [nt(one16, v[0, :, head_lanes(h)]) for h in every]
    rims = [nt(one16, jnp.concatenate([empty, rim[:, head_lanes(h)]], axis=0)) for h in every]
    values = []
    for h in every:
        whole = jnp.concatenate([rims[h], owns[h]], axis=1)
        conv = taps[0, h, 0:1] * owns[h]
        for j in range(1, count):
            conv = conv + (taps[0, h, j : j + 1] * keep[j - 1]) * pltpu.roll(whole, j, 1)[:, 128:]
        values.append((conv / (1.0 + jnp.exp(-conv))).astype(BF16))
    uvs = [nt(values[h], t[h]) for h in every]
    ends = [nn((uvs[h] * rows[24 + h : 25 + h]).astype(BF16), keys[h]) for h in every]
    for h in every:
        uv_out[h] = uvs[h].astype(BF16)
        mi_out[h] = (joined * m[h]).astype(BF16)
        mi_out[heads + h] = ends[h].astype(BF16)


def queries_body(q, k, rim, rows, cols_in, uk, uv, lw, local_out, reader_out, lw_out, lw_s):
    tokens = q.shape[1]
    features = q.shape[2]
    heads = uk.shape[0]
    first = lax.axis_index("ctx") == 0
    idf = rows[16:17]
    before = jnp.where(first, -1.0, rim[0:1, features : features + 128].astype(F32))
    joined = jnp.where(before[0:1, 127:128] == idf[:, 0:1], 1.0, 0.0)
    row_index = lax.broadcasted_iota(jnp.int32, (tokens, tokens), 0)
    col_index = lax.broadcasted_iota(jnp.int32, (tokens, tokens), 1)
    cols = cols_in[...]
    visible = (col_index <= row_index) & (cols[:, 24:25] == idf)
    lw_s[...] = jnp.zeros_like(lw_s)
    for h in range(heads):
        lw_s[h : h + 1] = lw[h]
    lw_out[...] = lw_s[...].T
    every = range(heads)
    qs = [q[0, :, head_lanes(h)] for h in every]
    qks = [nt(qs[h], k[0, :, head_lanes(h)]) for h in every]
    norms, readings = [], []
    for h in every:
        qf = qs[h].astype(F32)
        norms.append(lax.rsqrt(jnp.sum(qf * qf, axis=1, keepdims=True) + EPSILON))
        between = jnp.where(visible, jnp.exp(cols[:, h : h + 1] - rows[h : h + 1]), 0.0)
        readings.append((between * rows[8 + h : 9 + h] * (norms[h] * qks[h])).astype(BF16))
    both = [nt(readings[h], jnp.concatenate([uv[h], uk[h]], axis=0)) for h in every]
    for h in every:
        local_out[h] = both[h][:, 0:HEAD]
        reader = (cols[:, 16 + h : 17 + h] * norms[h]) * qs[h].astype(F32) - both[h][:, HEAD:]
        reader_out[h] = (joined * reader).astype(BF16)


def teacher_body(first_head, last_head, q, cols_in, own, r2, r4, x0, x2, x4, *refs):
    out, full, k_s, v_s, id_s, bias_s = refs[-6:]
    if first_head:
        out[0, :, 0 : first_head * HEAD] = refs[0][0, :, 0 : first_head * HEAD]
    tokens = q.shape[1]
    halves = tokens // 128
    index = lax.axis_index("ctx")
    odd = lax.rem(index, 2) == 1
    def place(slot, source):
        k_s[slot * tokens : (slot + 1) * tokens] = source[0:tokens]
        v_s[slot * tokens : (slot + 1) * tokens] = source[tokens : 2 * tokens]
        behind = 4 - slot
        valid = index >= behind
        names = source[2 * tokens : 2 * tokens + 16].astype(F32)
        for i in range(halves):
            at = (slot * halves + i) * 128
            id_s[:, at : at + 128] = jnp.where(valid, names[i : i + 1], -1.0)

    place(0, r4)
    place(2, r2)
    place(4, own)

    @pl.when(odd)
    def _():
        place(1, x2)
        place(3, x0)

    @pl.when(jnp.logical_not(odd))
    def _():
        place(1, x4)
        place(3, x2)

    width = 5 * tokens
    id_col = cols_in[:, 24:25]
    same = id_col == id_s[...]
    row_index = lax.broadcasted_iota(jnp.int32, (tokens, width), 0)
    col_index = lax.broadcasted_iota(jnp.int32, (tokens, width), 1) - 4 * tokens
    bias_s[...] = jnp.where(same & (col_index <= row_index), 0.0, MASKED)
    scale = math.log2(math.e) / math.sqrt(HEAD)
    span = width - (halves - 1) * 128
    tiles = [(h, r) for h in range(first_head, last_head) for r in range(halves)]

    def scores(h, r):
        return nt(q[0, r * 128 : (r + 1) * 128, head_lanes(h)], k_s[r * 128 : r * 128 + span])

    ahead = 2
    ss = [scores(*tile) for tile in tiles[:ahead]]
    for n, (h, r) in enumerate(tiles):
        if n + ahead < len(tiles):
            ss.append(scores(*tiles[n + ahead]))
        at = head_lanes(h - first_head)
        rows = slice(r * 128, (r + 1) * 128)
        cols = slice(r * 128, r * 128 + span)
        s = ss[n] * scale + bias_s[rows, cols]
        largest = jnp.max(s, axis=1, keepdims=True)
        w = jnp.exp2(s - largest)
        total = jnp.sum(w, axis=1, keepdims=True)
        o = nn(w.astype(BF16), v_s[cols]) / total
        full[rows, at] = o
        out[0, rows, head_lanes(h)] = o.astype(BF16)


def is_odd():
    return lax.rem(lax.axis_index("ctx"), 2) == 1


def chip_body(own, other, after, m_out, i_out):
    heads, rows, _ = i_out.shape
    every = range(heads)
    odd = is_odd()
    later_m = [jnp.where(odd, own[h], other[h]) for h in every]
    early_m = [jnp.where(odd, other[h], own[h]) for h in every]
    early_i = [jnp.where(odd, other[heads + h, rows:], own[heads + h, 0:rows]) for h in every]
    ms = [nn(early_m[h], later_m[h]) for h in every]
    ends = [nn(early_i[h], later_m[h]) for h in every]
    for h in every:
        later_i = jnp.where(odd, own[heads + h, rows:], other[heads + h, 0:rows])
        m_out[h] = ms[h].astype(BF16)
        i_out[h] = (ends[h] + later_i.astype(F32)).astype(BF16)


def join_body(m, i, arriving, out):
    every = range(m.shape[0])
    ends = [nn(arriving[h], m[h]) for h in every]
    for h in every:
        out[h] = (ends[h] + i[h].astype(F32)).astype(BF16)


def finish_body(mine, theirs, other, local, reader, gain, teachers, lw, out, sums, out_s, student_s, sems):
    heads = mine.shape[0]
    every = range(heads)
    odd = is_odd()
    states = []
    for h in every:
        a, b = mine[h], theirs[h]
        states.append(jnp.concatenate([jnp.where(odd, b, a), jnp.where(odd, a, b)], axis=0))
    steps = [nn(states[h], other[h]) for h in every]
    for h in every:
        step = (steps[h] + other[heads + h].astype(F32)).astype(BF16)
        states[h] = jnp.where(odd, step, states[h])
    half = lw.shape[0] // 2
    moves = []
    for r in range(2):
        rows = slice(r * half, (r + 1) * half)
        os = [local[h, rows] + nt(reader[h, rows], states[h]) for h in every]
        for h in every:
            mean = jnp.sum(os[h] * os[h], axis=1, keepdims=True) * (1.0 / HEAD)
            student = os[h] * lax.rsqrt(mean + EPSILON) * gain[:, head_lanes(h)]
            student_s[rows, head_lanes(h)] = student
            out_s[rows, head_lanes(h)] = student.astype(BF16)
        moves.append(pltpu.make_async_copy(out_s.at[rows], out.at[0, rows], sems.at[r]))
        moves[r].start()
    total = jnp.zeros(lw.shape, F32)
    for h in every:
        difference = student_s[:, head_lanes(h)] - teachers[:, head_lanes(h)]
        total = total + lw[:, h : h + 1] * (difference * difference)
    partial = jnp.sum(jnp.sum(total, axis=0, keepdims=True), axis=1, keepdims=True)
    sums[...] = jnp.broadcast_to(partial, sums.shape)
    for move in moves:
        move.wait()


def on_device(
    student_q,
    student_k,
    student_v,
    beta,
    log_decay,
    kernel,
    out_gain,
    teacher_q,
    teacher_k,
    teacher_v,
    segment_ids,
    loss_weight,
):
    _, tokens, features = student_q.shape
    heads = beta.shape[1]
    shards = lax.axis_size("ctx")
    everyone = shards * lax.axis_size("head") * lax.axis_size("dp")

    def rotated(block, distance):
        return lax.ppermute(block, "ctx", [(i, (i + distance) % shards) for i in range(shards)])

    def swapped(block):
        return lax.ppermute(block, "ctx", [(i, i ^ 1) for i in range(shards)])

    def by_head(block):
        return block.reshape(heads, 1, tokens)

    kv, rim = call(
        pack_body,
        [((2 * tokens + 16, HEAD), BF16), ((16, features + 128), BF16)],
        teacher_k,
        teacher_v,
        student_v,
        segment_ids,
        scratch=[((1, tokens), jnp.int32)],
        hbm=(0, 1, 2, 3),
        vmem=PACK_VMEM,
    )
    rim = rotated(rim, 1)
    r2 = rotated(kv, 2)
    x0 = swapped(kv)
    t, uk, m0, rows, cols = call(
        keys_body,
        [
            ((heads, tokens, tokens), BF16),
            ((heads, HEAD, tokens), BF16),
            ((heads, HEAD, HEAD), F32),
            ((32, tokens), F32),
            ((tokens, 128), F32),
        ],
        student_k,
        by_head(beta),
        by_head(log_decay),
        segment_ids,
        scratch=[
            ((2, 8, tokens), F32),
            ((heads, 3, tokens // 2, tokens // 2), BF16),
            ((2 * heads, 32, tokens // 2), F32),
            ((2 * heads, tokens // 2, tokens // 2), F32),
            ((heads, 1, tokens), F32),
            ((heads, 1, tokens), F32),
            ((1, tokens), jnp.int32),
        ],
        hbm=(1, 2, 3),
        flops=5 * 10**8,
    )
    r4 = rotated(r2, 2)
    mi, uv = call(
        values_body,
        [((2 * heads, HEAD, HEAD), BF16), ((heads, HEAD, tokens), BF16)],
        student_v,
        rim,
        kernel,
        rows,
        t,
        student_k,
        m0,
        r2,
        flops=2 * 10**8,
    )
    mi_other = swapped(mi)
    x2 = swapped(r2)
    local, reader, lw = call(
        queries_body,
        [
            ((heads, tokens, HEAD), F32),
            ((heads, tokens, HEAD), BF16),
            ((tokens, 128), F32),
        ],
        student_q,
        student_k,
        rim,
        rows,
        cols,
        uk,
        uv,
        by_head(loss_weight),
        scratch=[((128, tokens), F32)],
        flops=2 * 10**8,
    )
    m_chip, i_chip = call(
        chip_body,
        [((heads, HEAD, HEAD), BF16), ((heads, HEAD // 2, HEAD), BF16)],
        mi,
        mi_other,
        lw,
    )
    behind = rotated(i_chip, 2)
    x4 = swapped(r4)

    def attend(first_head, last_head, *earlier):
        count = last_head - first_head
        return call(
            functools.partial(teacher_body, first_head, last_head),
            [((1, tokens, features), BF16), ((tokens, count * HEAD), F32)],
            teacher_q,
            cols,
            kv,
            r2,
            r4,
            x0,
            x2,
            x4,
            *earlier,
            flops=count * 10**8,
            scratch=[
                ((5 * tokens, HEAD), BF16),
                ((5 * tokens, HEAD), BF16),
                ((1, 5 * tokens), F32),
                ((tokens, 5 * tokens), F32),
            ],
        )

    (joined,) = call(
        join_body, [((heads, HEAD // 2, HEAD), BF16)], m_chip, i_chip, behind
    )
    mine = rotated(joined, 2)
    teacher_out, teacher = attend(0, heads)
    mine, teacher = lax.optimization_barrier((mine, teacher))
    theirs = swapped(mine)
    student_out, sums = call(
        finish_body,
        [((1, tokens, features), BF16), ((everyone, 128), F32)],
        mine,
        theirs,
        mi_other,
        local,
        reader,
        out_gain.reshape(1, features),
        teacher,
        lw,
        scratch=[((tokens, features), BF16), ((tokens, features), F32)],
        hbm_out=(0,),
        copies=2,
    )
    gathered = lax.all_to_all(sums, ("ctx", "head", "dp"), 0, 0, tiled=True)
    loss = jnp.sum(gathered[:, 0]) / (everyone * heads * tokens * HEAD)
    return (student_out, teacher_out, loss)


def solution(mesh):
    placed = (
        P("dp", "ctx", "head"),
        P("dp", "ctx", "head"),
        P("dp", "ctx", "head"),
        P("dp", "head", "ctx"),
        P("dp", "head", "ctx"),
        P("dp", "head", None, "ctx"),
        P("head"),
        P("dp", "ctx", "head"),
        P("dp", "ctx", "head"),
        P("dp", "ctx", "head"),
        P("dp", "ctx"),
        P("dp", "head", "ctx"),
    )
    return jax.shard_map(
        on_device,
        mesh=mesh,
        in_specs=placed,
        out_specs=(P("dp", "ctx", "head"), P("dp", "ctx", "head"), P()),
        check_vma=False,
    )
```

```python
import functools
import math

import jax
import jax.numpy as jnp
from jax import lax
from jax.experimental import pallas as pl
from jax.experimental.pallas import tpu as pltpu
from jax.sharding import PartitionSpec as P

EPSILON = 1e-06
MASKED = -1e30
HEAD = 128
F32 = jnp.float32
BF16 = jnp.bfloat16
VMEM_BYTES = 32 * 1024 * 1024
PACK_VMEM = 62 * 1024 * 1024


def nn(a, b, precision=None):
    return lax.dot_general(
        a, b, (((1,), (0,)), ((), ())), precision=precision, preferred_element_type=F32
    )


def nt(a, b):
    return lax.dot_general(a, b, (((1,), (1,)), ((), ())), preferred_element_type=F32)


def tn(a, b):
    return lax.dot_general(a, b, (((0,), (0,)), ((), ())), preferred_element_type=F32)


def head_lanes(h):
    return slice(h * HEAD, (h + 1) * HEAD)


def call(body, outs, *args, scratch=(), hbm=(), hbm_out=(), copies=0, flops=0, vmem=VMEM_BYTES):
    buffers = [pltpu.VMEM(s, d) for s, d in scratch]
    copies = copies or len(hbm)
    if copies:
        buffers.append(pltpu.SemaphoreType.DMA((copies,)))
    return pl.pallas_call(
        body,
        out_shape=[jax.ShapeDtypeStruct(s, d) for s, d in outs],
        in_specs=[
            pl.BlockSpec(memory_space=pltpu.HBM if i in hbm else pltpu.VMEM)
            for i in range(len(args))
        ],
        out_specs=[
            pl.BlockSpec(memory_space=pltpu.HBM if i in hbm_out else pltpu.VMEM)
            for i in range(len(outs))
        ],
        scratch_shapes=buffers,
        compiler_params=pltpu.CompilerParams(vmem_limit_bytes=vmem),
        cost_estimate=pl.CostEstimate(flops=flops, bytes_accessed=0, transcendentals=0),
    )(*args)


def pack_body(tk, tv, sv, ids, kv, rim, id_s, sems):
    tokens = tk.shape[1]
    features = sv.shape[2]
    moves = [
        pltpu.make_async_copy(ids, id_s, sems.at[0]),
        pltpu.make_async_copy(
            sv.at[0, tokens - 16 : tokens, :], rim.at[:, 0:features], sems.at[1]
        ),
        pltpu.make_async_copy(tk.at[0], kv.at[0:tokens], sems.at[2]),
        pltpu.make_async_copy(tv.at[0], kv.at[tokens : 2 * tokens], sems.at[3]),
    ]
    for move in moves:
        move.start()
    moves[0].wait()
    idf = id_s[...].astype(F32)
    rows = lax.broadcasted_iota(jnp.int32, (16, 128), 0)
    block = jnp.zeros((16, 128), F32)
    for i in range(tokens // 128):
        block = jnp.where(rows == i, idf[:, i * 128 : (i + 1) * 128], block)
    kv[2 * tokens : 2 * tokens + 16] = block.astype(BF16)
    rim[:, features : features + 128] = jnp.broadcast_to(
        idf[:, tokens - 128 : tokens], (16, 128)
    ).astype(BF16)
    for move in moves[1:]:
        move.wait()


def eye(n):
    rows = lax.broadcasted_iota(jnp.int32, (n, n), 0)
    cols = lax.broadcasted_iota(jnp.int32, (n, n), 1)
    return jnp.where(rows == cols, 1.0, 0.0)


def keys_body(k, beta, decay, ids, t_out, uk_out, m_out, rows_out, cols_out, eight, a_s, c_s, t_s, beta_s, decay_s, id_s, sems):
    tokens = k.shape[1]
    heads = beta.shape[0]
    half = tokens // 2
    small = c_s.shape[1]
    moves = [
        pltpu.make_async_copy(source, target, sems.at[i])
        for i, (source, target) in enumerate(((beta, beta_s), (decay, decay_s), (ids, id_s)))
    ]
    for move in moves:
        move.start()
    lane = lax.broadcasted_iota(jnp.int32, (tokens, 128), 1)
    packed = jnp.zeros((tokens, 128), F32)
    for h in range(heads):
        kf = k[0, :, head_lanes(h)].astype(F32)
        norm = lax.rsqrt(jnp.sum(kf * kf, axis=1, keepdims=True) + EPSILON)
        packed = jnp.where(lane == h, norm, packed)
    r8 = packed.T[0:8]
    for move in moves:
        move.wait()
    idf = id_s[...].astype(F32)
    eight[...] = jnp.zeros_like(eight)
    for h in range(heads):
        eight[0, h : h + 1] = decay_s[h]
        eight[1, h : h + 1] = beta_s[h]
    row_index = lax.broadcasted_iota(jnp.int32, (tokens, tokens), 0)
    col_index = lax.broadcasted_iota(jnp.int32, (tokens, tokens), 1)
    upto = jnp.where(row_index <= col_index, 1.0, 0.0)
    run8 = nn(eight[0], upto, lax.Precision.HIGHEST)
    br8 = eight[1] * r8
    fs8 = jnp.where(idf == idf[:, 0:1], jnp.exp(run8), 0.0)
    fsr8 = fs8 * r8
    wend8 = (
        jnp.where(
            idf == idf[:, tokens - 1 : tokens],
            jnp.exp(run8[:, tokens - 1 : tokens] - run8),
            0.0,
        )
        * br8
    )
    ids8 = jnp.broadcast_to(idf, (8, tokens))
    rows_out[...] = jnp.concatenate([run8, br8, ids8, wend8], axis=0)
    stacked = jnp.concatenate([run8, r8, fs8, ids8, jnp.zeros((96, tokens), F32)], axis=0)
    cols = stacked.T
    cols_out[...] = cols

    rh = lax.broadcasted_iota(jnp.int32, (half, half), 0)
    ch = lax.broadcasted_iota(jnp.int32, (half, half), 1)
    below = ch < rh
    cl = lax.broadcasted_iota(jnp.int32, (small, half), 1)
    owns = [(cl // small) == i for i in range(half // small)]
    for h in range(heads):
        kh = k[0, :, head_lanes(h)]
        for at, (i, j) in enumerate(((0, 0), (1, 0), (1, 1))):
            ri, rj = slice(i * half, (i + 1) * half), slice(j * half, (j + 1) * half)
            kk = nt(kh[ri], kh[rj])
            seen = cols[ri, 24:25] == idf[:, rj]
            if i == j:
                seen = seen & below
            between = jnp.where(seen, jnp.exp(cols[ri, h : h + 1] - run8[h : h + 1, rj]), 0.0)
            a = between * br8[h : h + 1, rj] * (cols[ri, 8 + h : 9 + h] * kk)
            a_s[h, at] = a.astype(BF16)
            if i == j:
                c = jnp.zeros((small, half), F32)
                for n, own in enumerate(owns):
                    c = jnp.where(own, a[n * small : (n + 1) * small], c)
                c_s[2 * h + i] = c

    rs = lax.broadcasted_iota(jnp.int32, (small, half), 0)
    cs = cl % small
    blocks = [(h, b) for h in range(heads) for b in range(2)]
    inside = jnp.where((rh // small) == (ch // small), 1.0, 0.0)
    inside16 = inside.astype(BF16)

    def merges(r, c, bits):
        rb, cb = r >> bits, c >> bits
        return jnp.where(((rb & 1) == 1) & (cb == rb - 1), 1.0, 0.0)

    def spread(x):
        return jnp.concatenate([x] * (half // small), axis=0) * inside16

    unit = jnp.where(rs == cs, 1.0, 0.0)
    first = merges(rs, cs, 0)
    ts = [unit - c_s[n] * first for n in range(len(blocks))]
    for bits in range(1, (small - 1).bit_length()):
        mask = merges(rs, cs, bits)
        tb = [t.astype(BF16) for t in ts]
        ps = [nn((c_s[n] * mask).astype(BF16), spread(tb[n])) for n in range(len(blocks))]
        ts = [t - nn(tb[n], spread(ps[n].astype(BF16))) for n, t in enumerate(ts)]
    for n, t in enumerate(ts):
        t_s[n] = jnp.concatenate([t] * (half // small), axis=0) * inside
    for bits in range((small - 1).bit_length(), (half - 1).bit_length()):
        size = 1 << bits
        odd = [slice(i * size, (i + 1) * size) for i in range(1, half // size, 2)]
        mask = merges(rh, ch, bits).astype(BF16)
        tb = [t_s[n].astype(BF16) for n in range(len(blocks))]
        ps = [
            nn(jnp.concatenate([(a_s[h, 2 * b, r] * mask[r]) for r in odd], axis=0), tb[n])
            for n, (h, b) in enumerate(blocks)
        ]
        changes = []
        for n in range(len(blocks)):
            p = ps[n].astype(BF16)
            pieces = []
            for i in range(len(odd)):
                pieces += [jnp.zeros((size, half), BF16), p[i * size : (i + 1) * size]]
            changes.append(
                nn(
                    jnp.concatenate([tb[n][r] for r in odd], axis=0),
                    jnp.concatenate(pieces, axis=0),
                )
            )
        for n in range(len(blocks)):
            for i, r in enumerate(odd):
                t_s[n, r] = t_s[n, r] - changes[n][i * size : (i + 1) * size]
    tb = [t_s[n].astype(BF16) for n in range(len(blocks))]
    one = eye(HEAD)
    one16 = one.astype(BF16)
    keys = [k[0, :, head_lanes(h)] for h in range(heads)]
    xs = [nt(one16, keys[h]) for h in range(heads)]
    ps = [nn(a_s[h, 1], tb[2 * h]).astype(BF16) for h in range(heads)]
    t21 = [(-nn(tb[2 * h + 1], ps[h])).astype(BF16) for h in range(heads)]
    for h in range(heads):
        t_out[h, 0:half, 0:half] = tb[2 * h]
        t_out[h, half:tokens, half:tokens] = tb[2 * h + 1]
        t_out[h, 0:half, half:tokens] = jnp.zeros((half, half), BF16)
        t_out[h, half:tokens, 0:half] = t21[h]
    none = jnp.zeros((half, half), BF16)
    ts = [
        jnp.concatenate(
            [
                jnp.concatenate([tb[2 * h], none], axis=1),
                jnp.concatenate([t21[h], tb[2 * h + 1]], axis=1),
            ],
            axis=0,
        )
        for h in range(heads)
    ]
    uks = [nt((xs[h] * fsr8[h : h + 1]).astype(BF16), ts[h]) for h in range(heads)]
    ms = [nn((uks[h] * wend8[h : h + 1]).astype(BF16), keys[h]) for h in range(heads)]
    for h in range(heads):
        uk_out[h] = uks[h].astype(BF16)
        m_out[h] = one * fs8[h : h + 1, tokens - 1 : tokens] - ms[h]


def values_body(v, rim, taps, rows, t, k, m, after, mi_out, uv_out):
    features = v.shape[2]
    heads = taps.shape[1]
    count = taps.shape[2]
    first = lax.axis_index("ctx") == 0
    idf = rows[16:17]
    before = rim[0:1, features : features + 128].astype(F32)
    before = jnp.where(first, -1.0, before)
    longer = jnp.concatenate([before, idf], axis=1)
    keep = [
        jnp.where(pltpu.roll(longer, j, 1)[:, 128:] == idf, 1.0, 0.0) for j in range(1, count)
    ]
    joined = jnp.where(before[0:1, 127:128] == idf[:, 0:1], 1.0, 0.0)
    one16 = eye(HEAD).astype(BF16)
    empty = jnp.zeros((112, HEAD), BF16)
    every = range(heads)
    keys = [k[0, :, head_lanes(h)] for h in every]
    owns = [nt(one16, v[0, :, head_lanes(h)]) for h in every]
    rims = [nt(one16, jnp.concatenate([empty, rim[:, head_lanes(h)]], axis=0)) for h in every]
    values = []
    for h in every:
        whole = jnp.concatenate([rims[h], owns[h]], axis=1)
        conv = taps[0, h, 0:1] * owns[h]
        for j in range(1, count):
            conv = conv + (taps[0, h, j : j + 1] * keep[j - 1]) * pltpu.roll(whole, j, 1)[:, 128:]
        values.append((conv / (1.0 + jnp.exp(-conv))).astype(BF16))
    uvs = [nt(values[h], t[h]) for h in every]
    ends = [nn((uvs[h] * rows[24 + h : 25 + h]).astype(BF16), keys[h]) for h in every]
    for h in every:
        uv_out[h] = uvs[h].astype(BF16)
        mi_out[h] = (joined * m[h]).astype(BF16)
        mi_out[heads + h] = ends[h].astype(BF16)


def queries_body(q, k, rim, rows, cols_in, uk, uv, lw, local_out, reader_out, lw_out, lw_s):
    tokens = q.shape[1]
    features = q.shape[2]
    heads = uk.shape[0]
    first = lax.axis_index("ctx") == 0
    idf = rows[16:17]
    before = jnp.where(first, -1.0, rim[0:1, features : features + 128].astype(F32))
    joined = jnp.where(before[0:1, 127:128] == idf[:, 0:1], 1.0, 0.0)
    row_index = lax.broadcasted_iota(jnp.int32, (tokens, tokens), 0)
    col_index = lax.broadcasted_iota(jnp.int32, (tokens, tokens), 1)
    cols = cols_in[...]
    visible = (col_index <= row_index) & (cols[:, 24:25] == idf)
    lw_s[...] = jnp.zeros_like(lw_s)
    for h in range(heads):
        lw_s[h : h + 1] = lw[h]
    lw_out[...] = lw_s[...].T
    every = range(heads)
    qs = [q[0, :, head_lanes(h)] for h in every]
    qks = [nt(qs[h], k[0, :, head_lanes(h)]) for h in every]
    norms, readings = [], []
    for h in every:
        qf = qs[h].astype(F32)
        norms.append(lax.rsqrt(jnp.sum(qf * qf, axis=1, keepdims=True) + EPSILON))
        between = jnp.where(visible, jnp.exp(cols[:, h : h + 1] - rows[h : h + 1]), 0.0)
        readings.append((between * rows[8 + h : 9 + h] * (norms[h] * qks[h])).astype(BF16))
    both = [nt(readings[h], jnp.concatenate([uv[h], uk[h]], axis=0)) for h in every]
    for h in every:
        local_out[h] = both[h][:, 0:HEAD]
        reader = (cols[:, 16 + h : 17 + h] * norms[h]) * qs[h].astype(F32) - both[h][:, HEAD:]
        reader_out[h] = (joined * reader).astype(BF16)


def teacher_body(first_head, last_head, q, cols_in, own, r2, r4, x0, x2, x4, *refs):
    out, full, k_s, v_s, id_s, bias_s = refs[-6:]
    if first_head:
        out[0, :, 0 : first_head * HEAD] = refs[0][0, :, 0 : first_head * HEAD]
    tokens = q.shape[1]
    halves = tokens // 128
    index = lax.axis_index("ctx")
    odd = lax.rem(index, 2) == 1
    def place(slot, source):
        k_s[slot * tokens : (slot + 1) * tokens] = source[0:tokens]
        v_s[slot * tokens : (slot + 1) * tokens] = source[tokens : 2 * tokens]
        behind = 4 - slot
        valid = index >= behind
        names = source[2 * tokens : 2 * tokens + 16].astype(F32)
        for i in range(halves):
            at = (slot * halves + i) * 128
            id_s[:, at : at + 128] = jnp.where(valid, names[i : i + 1], -1.0)

    place(0, r4)
    place(2, r2)
    place(4, own)

    @pl.when(odd)
    def _():
        place(1, x2)
        place(3, x0)

    @pl.when(jnp.logical_not(odd))
    def _():
        place(1, x4)
        place(3, x2)

    width = 5 * tokens
    id_col = cols_in[:, 24:25]
    same = id_col == id_s[...]
    row_index = lax.broadcasted_iota(jnp.int32, (tokens, width), 0)
    col_index = lax.broadcasted_iota(jnp.int32, (tokens, width), 1) - 4 * tokens
    bias_s[...] = jnp.where(same & (col_index <= row_index), 0.0, MASKED)
    scale = math.log2(math.e) / math.sqrt(HEAD)
    span = width - (halves - 1) * 128
    tiles = [(h, r) for h in range(first_head, last_head) for r in range(halves)]

    def scores(h, r):
        return nt(q[0, r * 128 : (r + 1) * 128, head_lanes(h)], k_s[r * 128 : r * 128 + span])

    ahead = 2
    ss = [scores(*tile) for tile in tiles[:ahead]]
    for n, (h, r) in enumerate(tiles):
        if n + ahead < len(tiles):
            ss.append(scores(*tiles[n + ahead]))
        at = head_lanes(h - first_head)
        rows = slice(r * 128, (r + 1) * 128)
        cols = slice(r * 128, r * 128 + span)
        s = ss[n] * scale + bias_s[rows, cols]
        largest = jnp.max(s, axis=1, keepdims=True)
        w = jnp.exp2(s - largest)
        total = jnp.sum(w, axis=1, keepdims=True)
        o = nn(w.astype(BF16), v_s[cols]) / total
        full[rows, at] = o
        out[0, rows, head_lanes(h)] = o.astype(BF16)


def is_odd():
    return lax.rem(lax.axis_index("ctx"), 2) == 1


def chip_body(own, other, after, m_out, i_out):
    heads, rows, _ = i_out.shape
    every = range(heads)
    odd = is_odd()
    later_m = [jnp.where(odd, own[h], other[h]) for h in every]
    early_m = [jnp.where(odd, other[h], own[h]) for h in every]
    early_i = [jnp.where(odd, other[heads + h, rows:], own[heads + h, 0:rows]) for h in every]
    ms = [nn(early_m[h], later_m[h]) for h in every]
    ends = [nn(early_i[h], later_m[h]) for h in every]
    for h in every:
        later_i = jnp.where(odd, own[heads + h, rows:], other[heads + h, 0:rows])
        m_out[h] = ms[h].astype(BF16)
        i_out[h] = (ends[h] + later_i.astype(F32)).astype(BF16)


def join_body(m, i, arriving, out):
    every = range(m.shape[0])
    ends = [nn(arriving[h], m[h]) for h in every]
    for h in every:
        out[h] = (ends[h] + i[h].astype(F32)).astype(BF16)


def finish_body(mine, theirs, other, local, reader, gain, teachers, lw, out, sums, out_s, student_s, sems):
    heads = mine.shape[0]
    every = range(heads)
    odd = is_odd()
    states = []
    for h in every:
        a, b = mine[h], theirs[h]
        states.append(jnp.concatenate([jnp.where(odd, b, a), jnp.where(odd, a, b)], axis=0))
    steps = [nn(states[h], other[h]) for h in every]
    for h in every:
        step = (steps[h] + other[heads + h].astype(F32)).astype(BF16)
        states[h] = jnp.where(odd, step, states[h])
    half = lw.shape[0] // 2
    moves = []
    for r in range(2):
        rows = slice(r * half, (r + 1) * half)
        os = [local[h, rows] + nt(reader[h, rows], states[h]) for h in every]
        for h in every:
            mean = jnp.sum(os[h] * os[h], axis=1, keepdims=True) * (1.0 / HEAD)
            student = os[h] * lax.rsqrt(mean + EPSILON) * gain[:, head_lanes(h)]
            student_s[rows, head_lanes(h)] = student
            out_s[rows, head_lanes(h)] = student.astype(BF16)
        moves.append(pltpu.make_async_copy(out_s.at[rows], out.at[0, rows], sems.at[r]))
        moves[r].start()
    total = jnp.zeros(lw.shape, F32)
    for h in every:
        difference = student_s[:, head_lanes(h)] - teachers[:, head_lanes(h)]
        total = total + lw[:, h : h + 1] * (difference * difference)
    partial = jnp.sum(jnp.sum(total, axis=0, keepdims=True), axis=1, keepdims=True)
    sums[...] = jnp.broadcast_to(partial, sums.shape)
    for move in moves:
        move.wait()


def total_body(scale, parts, out):
    out[...] = jnp.sum(parts[:, 0:1], axis=0, keepdims=True) * scale


def on_device(
    student_q,
    student_k,
    student_v,
    beta,
    log_decay,
    kernel,
    out_gain,
    teacher_q,
    teacher_k,
    teacher_v,
    segment_ids,
    loss_weight,
):
    _, tokens, features = student_q.shape
    heads = beta.shape[1]
    shards = lax.axis_size("ctx")
    everyone = shards * lax.axis_size("head") * lax.axis_size("dp")

    def rotated(block, distance):
        return lax.ppermute(block, "ctx", [(i, (i + distance) % shards) for i in range(shards)])

    def swapped(block):
        return lax.ppermute(block, "ctx", [(i, i ^ 1) for i in range(shards)])

    def by_head(block):
        return block.reshape(heads, 1, tokens)

    kv, rim = call(
        pack_body,
        [((2 * tokens + 16, HEAD), BF16), ((16, features + 128), BF16)],
        teacher_k,
        teacher_v,
        student_v,
        segment_ids,
        scratch=[((1, tokens), jnp.int32)],
        hbm=(0, 1, 2, 3),
        vmem=PACK_VMEM,
    )
    rim = rotated(rim, 1)
    r2 = rotated(kv, 2)
    x0 = swapped(kv)
    t, uk, m0, rows, cols = call(
        keys_body,
        [
            ((heads, tokens, tokens), BF16),
            ((heads, HEAD, tokens), BF16),
            ((heads, HEAD, HEAD), F32),
            ((32, tokens), F32),
            ((tokens, 128), F32),
        ],
        student_k,
        by_head(beta),
        by_head(log_decay),
        segment_ids,
        scratch=[
            ((2, 8, tokens), F32),
            ((heads, 3, tokens // 2, tokens // 2), BF16),
            ((2 * heads, 32, tokens // 2), F32),
            ((2 * heads, tokens // 2, tokens // 2), F32),
            ((heads, 1, tokens), F32),
            ((heads, 1, tokens), F32),
            ((1, tokens), jnp.int32),
        ],
        hbm=(1, 2, 3),
        flops=5 * 10**8,
    )
    r4 = rotated(r2, 2)
    mi, uv = call(
        values_body,
        [((2 * heads, HEAD, HEAD), BF16), ((heads, HEAD, tokens), BF16)],
        student_v,
        rim,
        kernel,
        rows,
        t,
        student_k,
        m0,
        r2,
        flops=2 * 10**8,
    )
    mi_other = swapped(mi)
    x2 = swapped(r2)
    local, reader, lw = call(
        queries_body,
        [
            ((heads, tokens, HEAD), F32),
            ((heads, tokens, HEAD), BF16),
            ((tokens, 128), F32),
        ],
        student_q,
        student_k,
        rim,
        rows,
        cols,
        uk,
        uv,
        by_head(loss_weight),
        scratch=[((128, tokens), F32)],
        flops=2 * 10**8,
    )
    m_chip, i_chip = call(
        chip_body,
        [((heads, HEAD, HEAD), BF16), ((heads, HEAD // 2, HEAD), BF16)],
        mi,
        mi_other,
        lw,
    )
    behind = rotated(i_chip, 2)
    x4 = swapped(r4)

    def attend(first_head, last_head, *earlier):
        count = last_head - first_head
        return call(
            functools.partial(teacher_body, first_head, last_head),
            [((1, tokens, features), BF16), ((tokens, count * HEAD), F32)],
            teacher_q,
            cols,
            kv,
            r2,
            r4,
            x0,
            x2,
            x4,
            *earlier,
            flops=count * 10**8,
            scratch=[
                ((5 * tokens, HEAD), BF16),
                ((5 * tokens, HEAD), BF16),
                ((1, 5 * tokens), F32),
                ((tokens, 5 * tokens), F32),
            ],
        )

    (joined,) = call(
        join_body, [((heads, HEAD // 2, HEAD), BF16)], m_chip, i_chip, behind
    )
    mine = rotated(joined, 2)
    teacher_out, teacher = attend(0, heads)
    mine, teacher = lax.optimization_barrier((mine, teacher))
    theirs = swapped(mine)
    student_out, sums = call(
        finish_body,
        [((1, tokens, features), BF16), ((everyone, 128), F32)],
        mine,
        theirs,
        mi_other,
        local,
        reader,
        out_gain.reshape(1, features),
        teacher,
        lw,
        scratch=[((tokens, features), BF16), ((tokens, features), F32)],
        hbm_out=(0,),
        copies=2,
    )
    gathered = lax.all_to_all(sums, ("ctx", "head", "dp"), 0, 0, tiled=True)
    scale = 1.0 / (everyone * heads * tokens * HEAD)
    (loss,) = call(functools.partial(total_body, scale), [((1, 1), F32)], gathered)
    loss = loss.reshape(())
    return (student_out, teacher_out, loss)


def solution(mesh):
    placed = (
        P("dp", "ctx", "head"),
        P("dp", "ctx", "head"),
        P("dp", "ctx", "head"),
        P("dp", "head", "ctx"),
        P("dp", "head", "ctx"),
        P("dp", "head", None, "ctx"),
        P("head"),
        P("dp", "ctx", "head"),
        P("dp", "ctx", "head"),
        P("dp", "ctx", "head"),
        P("dp", "ctx"),
        P("dp", "head", "ctx"),
    )
    return jax.shard_map(
        on_device,
        mesh=mesh,
        in_specs=placed,
        out_specs=(P("dp", "ctx", "head"), P("dp", "ctx", "head"), P()),
        check_vma=False,
    )
```

```python
import functools
import math

import jax
import jax.numpy as jnp
from jax import lax
from jax.experimental import pallas as pl
from jax.experimental.pallas import tpu as pltpu
from jax.sharding import PartitionSpec as P

EPSILON = 1e-06
MASKED = -1e30
HEAD = 128
F32 = jnp.float32
BF16 = jnp.bfloat16
VMEM_BYTES = 32 * 1024 * 1024
PACK_VMEM = 62 * 1024 * 1024


def nn(a, b, precision=None):
    return lax.dot_general(
        a, b, (((1,), (0,)), ((), ())), precision=precision, preferred_element_type=F32
    )


def nt(a, b):
    return lax.dot_general(a, b, (((1,), (1,)), ((), ())), preferred_element_type=F32)


def tn(a, b):
    return lax.dot_general(a, b, (((0,), (0,)), ((), ())), preferred_element_type=F32)


def head_lanes(h):
    return slice(h * HEAD, (h + 1) * HEAD)


def call(body, outs, *args, scratch=(), hbm=(), hbm_out=(), copies=0, flops=0, vmem=VMEM_BYTES):
    buffers = [pltpu.VMEM(s, d) for s, d in scratch]
    copies = copies or len(hbm)
    if copies:
        buffers.append(pltpu.SemaphoreType.DMA((copies,)))
    return pl.pallas_call(
        body,
        out_shape=[jax.ShapeDtypeStruct(s, d) for s, d in outs],
        in_specs=[
            pl.BlockSpec(memory_space=pltpu.HBM if i in hbm else pltpu.VMEM)
            for i in range(len(args))
        ],
        out_specs=[
            pl.BlockSpec(memory_space=pltpu.HBM if i in hbm_out else pltpu.VMEM)
            for i in range(len(outs))
        ],
        scratch_shapes=buffers,
        compiler_params=pltpu.CompilerParams(vmem_limit_bytes=vmem),
        cost_estimate=pl.CostEstimate(flops=flops, bytes_accessed=0, transcendentals=0),
    )(*args)


def pack_body(tk, tv, sv, ids, kv, rim, id_s, sems):
    tokens = tk.shape[1]
    features = sv.shape[2]
    moves = [
        pltpu.make_async_copy(ids, id_s, sems.at[0]),
        pltpu.make_async_copy(
            sv.at[0, tokens - 16 : tokens, :], rim.at[:, 0:features], sems.at[1]
        ),
        pltpu.make_async_copy(tk.at[0], kv.at[0:tokens], sems.at[2]),
        pltpu.make_async_copy(tv.at[0], kv.at[tokens : 2 * tokens], sems.at[3]),
    ]
    for move in moves:
        move.start()
    moves[0].wait()
    idf = id_s[...].astype(F32)
    rows = lax.broadcasted_iota(jnp.int32, (16, 128), 0)
    block = jnp.zeros((16, 128), F32)
    for i in range(tokens // 128):
        block = jnp.where(rows == i, idf[:, i * 128 : (i + 1) * 128], block)
    kv[2 * tokens : 2 * tokens + 16] = block.astype(BF16)
    rim[:, features : features + 128] = jnp.broadcast_to(
        idf[:, tokens - 128 : tokens], (16, 128)
    ).astype(BF16)
    for move in moves[1:]:
        move.wait()


def is_odd():
    return lax.rem(lax.axis_index("ctx"), 2) == 1


def eye(n):
    rows = lax.broadcasted_iota(jnp.int32, (n, n), 0)
    cols = lax.broadcasted_iota(jnp.int32, (n, n), 1)
    return jnp.where(rows == cols, 1.0, 0.0)


def keys_body(k, beta, decay, ids, t_out, uk_out, m_out, rows_out, cols_out, eight, a_s, c_s, t_s, beta_s, decay_s, id_s, sems):
    tokens = k.shape[1]
    heads = beta.shape[0]
    half = tokens // 2
    small = c_s.shape[1]
    moves = [
        pltpu.make_async_copy(source, target, sems.at[i])
        for i, (source, target) in enumerate(((beta, beta_s), (decay, decay_s), (ids, id_s)))
    ]
    for move in moves:
        move.start()
    lane = lax.broadcasted_iota(jnp.int32, (tokens, 128), 1)
    packed = jnp.zeros((tokens, 128), F32)
    for h in range(heads):
        kf = k[0, :, head_lanes(h)].astype(F32)
        norm = lax.rsqrt(jnp.sum(kf * kf, axis=1, keepdims=True) + EPSILON)
        packed = jnp.where(lane == h, norm, packed)
    r8 = packed.T[0:8]
    for move in moves:
        move.wait()
    idf = id_s[...].astype(F32)
    eight[...] = jnp.zeros_like(eight)
    for h in range(heads):
        eight[0, h : h + 1] = decay_s[h]
        eight[1, h : h + 1] = beta_s[h]
    row_index = lax.broadcasted_iota(jnp.int32, (tokens, tokens), 0)
    col_index = lax.broadcasted_iota(jnp.int32, (tokens, tokens), 1)
    upto = jnp.where(row_index <= col_index, 1.0, 0.0)
    run8 = nn(eight[0], upto, lax.Precision.HIGHEST)
    br8 = eight[1] * r8
    fs8 = jnp.where(idf == idf[:, 0:1], jnp.exp(run8), 0.0)
    fsr8 = fs8 * r8
    wend8 = (
        jnp.where(
            idf == idf[:, tokens - 1 : tokens],
            jnp.exp(run8[:, tokens - 1 : tokens] - run8),
            0.0,
        )
        * br8
    )
    ids8 = jnp.broadcast_to(idf, (8, tokens))
    rows_out[...] = jnp.concatenate([run8, br8, ids8, wend8], axis=0)
    stacked = jnp.concatenate([run8, r8, fs8, ids8, jnp.zeros((96, tokens), F32)], axis=0)
    cols = stacked.T
    cols_out[...] = cols

    rh = lax.broadcasted_iota(jnp.int32, (half, half), 0)
    ch = lax.broadcasted_iota(jnp.int32, (half, half), 1)
    below = ch < rh
    cl = lax.broadcasted_iota(jnp.int32, (small, half), 1)
    owns = [(cl // small) == i for i in range(half // small)]
    for h in range(heads):
        kh = k[0, :, head_lanes(h)]
        for at, (i, j) in enumerate(((0, 0), (1, 0), (1, 1))):
            ri, rj = slice(i * half, (i + 1) * half), slice(j * half, (j + 1) * half)
            kk = nt(kh[ri], kh[rj])
            seen = cols[ri, 24:25] == idf[:, rj]
            if i == j:
                seen = seen & below
            between = jnp.where(seen, jnp.exp(cols[ri, h : h + 1] - run8[h : h + 1, rj]), 0.0)
            a = between * br8[h : h + 1, rj] * (cols[ri, 8 + h : 9 + h] * kk)
            a_s[h, at] = a.astype(BF16)
            if i == j:
                c = jnp.zeros((small, half), F32)
                for n, own in enumerate(owns):
                    c = jnp.where(own, a[n * small : (n + 1) * small], c)
                c_s[2 * h + i] = c

    rs = lax.broadcasted_iota(jnp.int32, (small, half), 0)
    cs = cl % small
    blocks = [(h, b) for h in range(heads) for b in range(2)]
    inside = jnp.where((rh // small) == (ch // small), 1.0, 0.0)
    inside16 = inside.astype(BF16)

    def merges(r, c, bits):
        rb, cb = r >> bits, c >> bits
        return jnp.where(((rb & 1) == 1) & (cb == rb - 1), 1.0, 0.0)

    def spread(x):
        return jnp.concatenate([x] * (half // small), axis=0) * inside16

    unit = jnp.where(rs == cs, 1.0, 0.0)
    first = merges(rs, cs, 0)
    ts = [unit - c_s[n] * first for n in range(len(blocks))]
    for bits in range(1, (small - 1).bit_length()):
        mask = merges(rs, cs, bits)
        tb = [t.astype(BF16) for t in ts]
        ps = [nn((c_s[n] * mask).astype(BF16), spread(tb[n])) for n in range(len(blocks))]
        ts = [t - nn(tb[n], spread(ps[n].astype(BF16))) for n, t in enumerate(ts)]
    for n, t in enumerate(ts):
        t_s[n] = jnp.concatenate([t] * (half // small), axis=0) * inside
    for bits in range((small - 1).bit_length(), (half - 1).bit_length()):
        size = 1 << bits
        odd = [slice(i * size, (i + 1) * size) for i in range(1, half // size, 2)]
        mask = merges(rh, ch, bits).astype(BF16)
        tb = [t_s[n].astype(BF16) for n in range(len(blocks))]
        ps = [
            nn(jnp.concatenate([(a_s[h, 2 * b, r] * mask[r]) for r in odd], axis=0), tb[n])
            for n, (h, b) in enumerate(blocks)
        ]
        changes = []
        for n in range(len(blocks)):
            p = ps[n].astype(BF16)
            pieces = []
            for i in range(len(odd)):
                pieces += [jnp.zeros((size, half), BF16), p[i * size : (i + 1) * size]]
            changes.append(
                nn(
                    jnp.concatenate([tb[n][r] for r in odd], axis=0),
                    jnp.concatenate(pieces, axis=0),
                )
            )
        for n in range(len(blocks)):
            for i, r in enumerate(odd):
                t_s[n, r] = t_s[n, r] - changes[n][i * size : (i + 1) * size]
    tb = [t_s[n].astype(BF16) for n in range(len(blocks))]
    one = eye(HEAD)
    one16 = one.astype(BF16)
    keys = [k[0, :, head_lanes(h)] for h in range(heads)]
    xs = [nt(one16, keys[h]) for h in range(heads)]
    ps = [nn(a_s[h, 1], tb[2 * h]).astype(BF16) for h in range(heads)]
    t21 = [(-nn(tb[2 * h + 1], ps[h])).astype(BF16) for h in range(heads)]
    for h in range(heads):
        t_out[h, 0:half, 0:half] = tb[2 * h]
        t_out[h, half:tokens, half:tokens] = tb[2 * h + 1]
        t_out[h, 0:half, half:tokens] = jnp.zeros((half, half), BF16)
        t_out[h, half:tokens, 0:half] = t21[h]
    none = jnp.zeros((half, half), BF16)
    ts = [
        jnp.concatenate(
            [
                jnp.concatenate([tb[2 * h], none], axis=1),
                jnp.concatenate([t21[h], tb[2 * h + 1]], axis=1),
            ],
            axis=0,
        )
        for h in range(heads)
    ]
    uks = [nt((xs[h] * fsr8[h : h + 1]).astype(BF16), ts[h]) for h in range(heads)]
    ms = [nn((uks[h] * wend8[h : h + 1]).astype(BF16), keys[h]) for h in range(heads)]
    for h in range(heads):
        uk_out[h] = uks[h].astype(BF16)
        m_out[h] = one * fs8[h : h + 1, tokens - 1 : tokens] - ms[h]


def values_body(v, rim, taps, rows, t, k, m, after, mi_out, uv_out):
    features = v.shape[2]
    heads = taps.shape[1]
    count = taps.shape[2]
    first = lax.axis_index("ctx") == 0
    idf = rows[16:17]
    before = rim[0:1, features : features + 128].astype(F32)
    before = jnp.where(first, -1.0, before)
    longer = jnp.concatenate([before, idf], axis=1)
    keep = [
        jnp.where(pltpu.roll(longer, j, 1)[:, 128:] == idf, 1.0, 0.0) for j in range(1, count)
    ]
    joined = jnp.where(before[0:1, 127:128] == idf[:, 0:1], 1.0, 0.0)
    one16 = eye(HEAD).astype(BF16)
    empty = jnp.zeros((112, HEAD), BF16)
    every = range(heads)
    keys = [k[0, :, head_lanes(h)] for h in every]
    owns = [nt(one16, v[0, :, head_lanes(h)]) for h in every]
    rims = [nt(one16, jnp.concatenate([empty, rim[:, head_lanes(h)]], axis=0)) for h in every]
    values = []
    for h in every:
        whole = jnp.concatenate([rims[h], owns[h]], axis=1)
        conv = taps[0, h, 0:1] * owns[h]
        for j in range(1, count):
            conv = conv + (taps[0, h, j : j + 1] * keep[j - 1]) * pltpu.roll(whole, j, 1)[:, 128:]
        values.append((conv / (1.0 + jnp.exp(-conv))).astype(BF16))
    uvs = [nt(values[h], t[h]) for h in every]
    ends = [nn((uvs[h] * rows[24 + h : 25 + h]).astype(BF16), keys[h]) for h in every]
    for h in every:
        uv_out[h] = uvs[h].astype(BF16)
        mi_out[h] = (joined * m[h]).astype(BF16)
        mi_out[heads + h] = ends[h].astype(BF16)


def queries_body(q, k, rim, rows, cols_in, uk, uv, other, lw, local_out, reader_out, lw_out, lw_s):
    tokens = q.shape[1]
    features = q.shape[2]
    heads = uk.shape[0]
    first = lax.axis_index("ctx") == 0
    idf = rows[16:17]
    before = jnp.where(first, -1.0, rim[0:1, features : features + 128].astype(F32))
    joined = jnp.where(before[0:1, 127:128] == idf[:, 0:1], 1.0, 0.0)
    row_index = lax.broadcasted_iota(jnp.int32, (tokens, tokens), 0)
    col_index = lax.broadcasted_iota(jnp.int32, (tokens, tokens), 1)
    cols = cols_in[...]
    visible = (col_index <= row_index) & (cols[:, 24:25] == idf)
    lw_s[...] = jnp.zeros_like(lw_s)
    for h in range(heads):
        lw_s[h : h + 1] = lw[h]
    lw_out[...] = lw_s[...].T
    every = range(heads)
    qs = [q[0, :, head_lanes(h)] for h in every]
    qks = [nt(qs[h], k[0, :, head_lanes(h)]) for h in every]
    norms, readings = [], []
    for h in every:
        qf = qs[h].astype(F32)
        norms.append(lax.rsqrt(jnp.sum(qf * qf, axis=1, keepdims=True) + EPSILON))
        between = jnp.where(visible, jnp.exp(cols[:, h : h + 1] - rows[h : h + 1]), 0.0)
        readings.append((between * rows[8 + h : 9 + h] * (norms[h] * qks[h])).astype(BF16))
    both = [nt(readings[h], jnp.concatenate([uv[h], uk[h]], axis=0)) for h in every]
    readers = []
    for h in every:
        reader = (cols[:, 16 + h : 17 + h] * norms[h]) * qs[h].astype(F32) - both[h][:, HEAD:]
        readers.append((joined * reader).astype(BF16))
    odd = is_odd()
    steps = [
        nt(readers[h], jnp.concatenate([other[h], other[heads + h]], axis=0)) for h in every
    ]
    for h in every:
        local_out[h] = both[h][:, 0:HEAD] + jnp.where(odd, steps[h][:, HEAD:], 0.0)
        reader_out[h] = jnp.where(odd, steps[h][:, 0:HEAD].astype(BF16), readers[h])


def teacher_body(first_head, last_head, q, cols_in, own, r2, r4, x0, x2, x4, *refs):
    out, full, k_s, v_s, id_s, bias_s = refs[-6:]
    if first_head:
        out[0, :, 0 : first_head * HEAD] = refs[0][0, :, 0 : first_head * HEAD]
    tokens = q.shape[1]
    halves = tokens // 128
    index = lax.axis_index("ctx")
    odd = lax.rem(index, 2) == 1
    def place(slot, source):
        k_s[slot * tokens : (slot + 1) * tokens] = source[0:tokens]
        v_s[slot * tokens : (slot + 1) * tokens] = source[tokens : 2 * tokens]
        behind = 4 - slot
        valid = index >= behind
        names = source[2 * tokens : 2 * tokens + 16].astype(F32)
        for i in range(halves):
            at = (slot * halves + i) * 128
            id_s[:, at : at + 128] = jnp.where(valid, names[i : i + 1], -1.0)

    place(0, r4)
    place(2, r2)
    place(4, own)

    @pl.when(odd)
    def _():
        place(1, x2)
        place(3, x0)

    @pl.when(jnp.logical_not(odd))
    def _():
        place(1, x4)
        place(3, x2)

    width = 5 * tokens
    id_col = cols_in[:, 24:25]
    same = id_col == id_s[...]
    row_index = lax.broadcasted_iota(jnp.int32, (tokens, width), 0)
    col_index = lax.broadcasted_iota(jnp.int32, (tokens, width), 1) - 4 * tokens
    bias_s[...] = jnp.where(same & (col_index <= row_index), 0.0, MASKED)
    scale = math.log2(math.e) / math.sqrt(HEAD)
    span = width - (halves - 1) * 128
    tiles = [(h, r) for h in range(first_head, last_head) for r in range(halves)]

    def scores(h, r):
        return nt(q[0, r * 128 : (r + 1) * 128, head_lanes(h)], k_s[r * 128 : r * 128 + span])

    ahead = 2
    ss = [scores(*tile) for tile in tiles[:ahead]]
    for n, (h, r) in enumerate(tiles):
        if n + ahead < len(tiles):
            ss.append(scores(*tiles[n + ahead]))
        at = head_lanes(h - first_head)
        rows = slice(r * 128, (r + 1) * 128)
        cols = slice(r * 128, r * 128 + span)
        s = ss[n] * scale + bias_s[rows, cols]
        largest = jnp.max(s, axis=1, keepdims=True)
        w = jnp.exp2(s - largest)
        total = jnp.sum(w, axis=1, keepdims=True)
        o = nn(w.astype(BF16), v_s[cols]) / total
        full[rows, at] = o
        out[0, rows, head_lanes(h)] = o.astype(BF16)


def chip_body(own, other, m_out, i_out):
    heads, rows, _ = i_out.shape
    every = range(heads)
    odd = is_odd()
    later_m = [jnp.where(odd, own[h], other[h]) for h in every]
    early_m = [jnp.where(odd, other[h], own[h]) for h in every]
    early_i = [jnp.where(odd, other[heads + h, rows:], own[heads + h, 0:rows]) for h in every]
    ms = [nn(early_m[h], later_m[h]) for h in every]
    ends = [nn(early_i[h], later_m[h]) for h in every]
    for h in every:
        later_i = jnp.where(odd, own[heads + h, rows:], other[heads + h, 0:rows])
        m_out[h] = ms[h].astype(BF16)
        i_out[h] = (ends[h] + later_i.astype(F32)).astype(BF16)


def join_body(m, i, arriving, after, out):
    every = range(m.shape[0])
    ends = [nn(arriving[h], m[h]) for h in every]
    for h in every:
        out[h] = (ends[h] + i[h].astype(F32)).astype(BF16)


def finish_body(mine, theirs, local, reader, gain, teachers, lw, out, sums, out_s, student_s, sems):
    heads = mine.shape[0]
    every = range(heads)
    odd = is_odd()
    states = []
    for h in every:
        a, b = mine[h], theirs[h]
        states.append(jnp.concatenate([jnp.where(odd, b, a), jnp.where(odd, a, b)], axis=0))
    half = lw.shape[0] // 2
    moves = []
    for r in range(2):
        rows = slice(r * half, (r + 1) * half)
        os = [local[h, rows] + nt(reader[h, rows], states[h]) for h in every]
        for h in every:
            mean = jnp.sum(os[h] * os[h], axis=1, keepdims=True) * (1.0 / HEAD)
            student = os[h] * lax.rsqrt(mean + EPSILON) * gain[:, head_lanes(h)]
            student_s[rows, head_lanes(h)] = student
            out_s[rows, head_lanes(h)] = student.astype(BF16)
        moves.append(pltpu.make_async_copy(out_s.at[rows], out.at[0, rows], sems.at[r]))
        moves[r].start()
    total = jnp.zeros(lw.shape, F32)
    for h in every:
        difference = student_s[:, head_lanes(h)] - teachers[:, head_lanes(h)]
        total = total + lw[:, h : h + 1] * (difference * difference)
    partial = jnp.sum(jnp.sum(total, axis=0, keepdims=True), axis=1, keepdims=True)
    sums[...] = jnp.broadcast_to(partial, sums.shape)
    for move in moves:
        move.wait()


def total_body(scale, parts, out):
    out[...] = jnp.sum(parts[:, 0:1], axis=0, keepdims=True) * scale


def on_device(
    student_q,
    student_k,
    student_v,
    beta,
    log_decay,
    kernel,
    out_gain,
    teacher_q,
    teacher_k,
    teacher_v,
    segment_ids,
    loss_weight,
):
    _, tokens, features = student_q.shape
    heads = beta.shape[1]
    shards = lax.axis_size("ctx")
    everyone = shards * lax.axis_size("head") * lax.axis_size("dp")

    def rotated(block, distance):
        return lax.ppermute(block, "ctx", [(i, (i + distance) % shards) for i in range(shards)])

    def swapped(block):
        return lax.ppermute(block, "ctx", [(i, i ^ 1) for i in range(shards)])

    def by_head(block):
        return block.reshape(heads, 1, tokens)

    kv, rim = call(
        pack_body,
        [((2 * tokens + 16, HEAD), BF16), ((16, features + 128), BF16)],
        teacher_k,
        teacher_v,
        student_v,
        segment_ids,
        scratch=[((1, tokens), jnp.int32)],
        hbm=(0, 1, 2, 3),
        vmem=PACK_VMEM,
    )
    rim = rotated(rim, 1)
    r2 = rotated(kv, 2)
    x0 = swapped(kv)
    t, uk, m0, rows, cols = call(
        keys_body,
        [
            ((heads, tokens, tokens), BF16),
            ((heads, HEAD, tokens), BF16),
            ((heads, HEAD, HEAD), F32),
            ((32, tokens), F32),
            ((tokens, 128), F32),
        ],
        student_k,
        by_head(beta),
        by_head(log_decay),
        segment_ids,
        scratch=[
            ((2, 8, tokens), F32),
            ((heads, 3, tokens // 2, tokens // 2), BF16),
            ((2 * heads, 32, tokens // 2), F32),
            ((2 * heads, tokens // 2, tokens // 2), F32),
            ((heads, 1, tokens), F32),
            ((heads, 1, tokens), F32),
            ((1, tokens), jnp.int32),
        ],
        hbm=(1, 2, 3),
        flops=5 * 10**8,
    )
    r4 = rotated(r2, 2)
    mi, uv = call(
        values_body,
        [((2 * heads, HEAD, HEAD), BF16), ((heads, HEAD, tokens), BF16)],
        student_v,
        rim,
        kernel,
        rows,
        t,
        student_k,
        m0,
        r2,
        flops=2 * 10**8,
    )
    mi_other = swapped(mi)
    x2 = swapped(r2)
    local, reader, lw = call(
        queries_body,
        [
            ((heads, tokens, HEAD), F32),
            ((heads, tokens, HEAD), BF16),
            ((tokens, 128), F32),
        ],
        student_q,
        student_k,
        rim,
        rows,
        cols,
        uk,
        uv,
        mi_other,
        by_head(loss_weight),
        scratch=[((128, tokens), F32)],
        flops=2 * 10**8,
    )
    m_chip, i_chip = call(
        chip_body,
        [((heads, HEAD, HEAD), BF16), ((heads, HEAD // 2, HEAD), BF16)],
        mi,
        mi_other,
    )
    behind = rotated(i_chip, 2)
    x4 = swapped(r4)

    def attend(first_head, last_head, *earlier):
        count = last_head - first_head
        return call(
            functools.partial(teacher_body, first_head, last_head),
            [((1, tokens, features), BF16), ((tokens, count * HEAD), F32)],
            teacher_q,
            cols,
            kv,
            r2,
            r4,
            x0,
            x2,
            x4,
            *earlier,
            flops=count * 10**8,
            scratch=[
                ((5 * tokens, HEAD), BF16),
                ((5 * tokens, HEAD), BF16),
                ((1, 5 * tokens), F32),
                ((tokens, 5 * tokens), F32),
            ],
        )

    (joined,) = call(
        join_body, [((heads, HEAD // 2, HEAD), BF16)], m_chip, i_chip, behind, lw
    )
    mine = rotated(joined, 2)
    teacher_out, teacher = attend(0, heads)
    mine, teacher = lax.optimization_barrier((mine, teacher))
    theirs = swapped(mine)
    student_out, sums = call(
        finish_body,
        [((1, tokens, features), BF16), ((everyone, 128), F32)],
        mine,
        theirs,
        local,
        reader,
        out_gain.reshape(1, features),
        teacher,
        lw,
        scratch=[((tokens, features), BF16), ((tokens, features), F32)],
        hbm_out=(0,),
        copies=2,
    )
    gathered = lax.all_to_all(sums, ("ctx", "head", "dp"), 0, 0, tiled=True)
    scale = 1.0 / (everyone * heads * tokens * HEAD)
    (loss,) = call(functools.partial(total_body, scale), [((1, 1), F32)], gathered)
    loss = loss.reshape(())
    return (student_out, teacher_out, loss)


def solution(mesh):
    placed = (
        P("dp", "ctx", "head"),
        P("dp", "ctx", "head"),
        P("dp", "ctx", "head"),
        P("dp", "head", "ctx"),
        P("dp", "head", "ctx"),
        P("dp", "head", None, "ctx"),
        P("head"),
        P("dp", "ctx", "head"),
        P("dp", "ctx", "head"),
        P("dp", "ctx", "head"),
        P("dp", "ctx"),
        P("dp", "head", "ctx"),
    )
    return jax.shard_map(
        on_device,
        mesh=mesh,
        in_specs=placed,
        out_specs=(P("dp", "ctx", "head"), P("dp", "ctx", "head"), P()),
        check_vma=False,
    )
```
